128 devices in a mesh: ctx: 32 (over x_hi, y, z), rep: 4 (over x_lo, core).
Axes of the slice: x: 4 (x_hi: 2, x_lo: 2; x = x_hi * 2 + x_lo), y: 4, z: 4, core: 2. Of those that a mesh axis runs over, the one named last changes fastest.
Arguments:
- stream: bfloat16 [4, 16384, 1536], P('rep', 'ctx'), may hold values from -6 to 6
- norm_gain_vector: float32 [1536], replicated, may hold values from 0.1 to 1.9
- conv_kernel: bfloat16 [3, 1536, 768], replicated, may hold values from -0.09375 to 0.09375
- point_kernel: bfloat16 [768, 1536], replicated, may hold values from -0.21875 to 0.21875
- out_grad: bfloat16 [4, 16384, 1536], P('rep', 'ctx'), may hold values from -6 to 6
Outputs:
- stream_out: bfloat16 [4, 16384, 1536], P('rep', 'ctx')
- stream_grad: bfloat16 [4, 16384, 1536], P('rep', 'ctx')
- kernel_grad: float32 [3, 1536, 768], P(None, 'ctx')
- point_grad: float32 [768, 1536], P(None, 'ctx')
- gain_grad: float32 [1536], P('ctx')
The draws below stay inside these ranges and needn't reach their ends.
All inputs are finite; a program needn't handle non-finite values.
Results may differ from the reference program's by a relative error of at most 0.0054.
Values may be sent and summed in bfloat16 or wider, within the bound.
No kernel may reach another device: no remote copies, remote signals or barrier semaphores. Data moves between devices by JAX's collectives and lax.ppermute only.
A program may use at most 128 MiB of HBM per device.

```python
import jax
import jax.numpy as jnp
from jax import lax

C = 1536
H = 768
TAPS = 3
LOOP = 16384
DILATION_STEP = 4096
SAMPLES = 4


def with_spikes(entries, stream_key, source, target, blocks, factor):
    def block_of(dim):
        return (jnp.arange(entries.shape[dim]) // (entries.shape[dim] // blocks)).reshape((-1,) + (1,) * (entries.ndim - 1 - dim))

    first = jax.random.permutation(stream_key, blocks)[block_of(target)]
    other_side = (block_of(target) + blocks // 2) % blocks
    return jnp.where((block_of(source) == first) | (block_of(source) == other_side), factor * entries, entries)


def level_of(rng, extent, pieces, least, largest):
    def one(dim, blocks):
        heights = jax.random.uniform(jax.random.fold_in(jax.random.fold_in(rng, 6), dim), (blocks,), jnp.float32, least / len(pieces), largest / len(pieces))
        return jnp.repeat(jnp.exp(heights), extent[dim] // blocks).reshape((-1,) + (1,) * (len(extent) - dim - 1))

    factor_of = one(*pieces[0])
    for cut in pieces[1:]:
        factor_of = factor_of * one(*cut)
    return factor_of


def normal_values(stream_key, dims, scale, reach, split=(), held_as=jnp.bfloat16):
    entries = jax.random.normal(stream_key, dims, jnp.float32) * scale
    if len(split) > 0:
        entries = level_of(stream_key, dims, split, -0.22, 0.18) * entries
    return jnp.clip(entries, min=-reach, max=reach).astype(held_as)


def gaussian_with(key, shape, width, reach, cuts, heavy, held_as=jnp.bfloat16):
    result = width * jax.random.normal(key, shape, jnp.float32)
    if cuts:
        result = result * level_of(key, shape, cuts, -0.22, 0.18)
    return jnp.clip(with_spikes(result, jax.random.fold_in(key, 3), *heavy), -reach, reach).astype(held_as)


def setup_inputs(seed: int = 0) -> dict:
    arg_keys = jax.random.split(jax.random.key(seed), 6)
    stream = normal_values(arg_keys[0], (SAMPLES, LOOP, C), 1.0, 6.0, ((0, 4), (1, 32)))
    norm_gain_vector = jnp.clip(1.0 + 0.18 * jax.random.normal(arg_keys[1], (C,), jnp.float32), 0.1, 1.9)
    conv_kernel = normal_values(arg_keys[2], (TAPS, C, H), (3 * C) ** -0.5, 0.09375)
    point_kernel = normal_values(arg_keys[3], (H, C), H ** -0.5, 0.21875)
    out_grad = gaussian_with(arg_keys[4], (SAMPLES, LOOP, C), 1.0, 6.0, ((0, 4), (1, 32)), (1, 2, 32, 2.75))
    return {"stream": stream, "norm_gain_vector": norm_gain_vector, "conv_kernel": conv_kernel, "point_kernel": point_kernel, "out_grad": out_grad}


def gelu_slope(value):
    return jax.jvp(jax.nn.gelu, (value,), (jnp.ones_like(value),))[1]

def contract_rows(left, right):
    return lax.dot_general(left, right, (((0,), (0,)), ((), ())), preferred_element_type=jnp.float32)

def contract_cols(left, right):
    return lax.dot_general(left, right, (((1,), (1,)), ((), ())), preferred_element_type=jnp.float32)

def one_sample(carry, inputs):
    stream, out_grad, norm_gain_vector, conv_kernel, point_kernel = (inputs[0], inputs[1], carry[3], carry[4], carry[5])
    complete_input = stream.astype(jnp.float32)
    root_mean_square = jnp.sqrt(lax.optimization_barrier(jnp.mean(complete_input * complete_input, axis=-1, keepdims=True)) + 1e-06)
    unit_norm_input = complete_input / root_mean_square
    normalized_input = unit_norm_input * norm_gain_vector
    activation_value = jax.nn.gelu(normalized_input).astype(jnp.bfloat16)
    forward_neighbor = jnp.roll(activation_value, -DILATION_STEP, axis=0)
    backward_neighbor = jnp.roll(activation_value, DILATION_STEP, axis=0)
    pre = jnp.dot(activation_value, conv_kernel[1], preferred_element_type=jnp.float32)
    pre = pre + jnp.dot(forward_neighbor, conv_kernel[2], preferred_element_type=jnp.float32)
    pre = pre + jnp.dot(backward_neighbor, conv_kernel[0], preferred_element_type=jnp.float32)
    mid = jax.nn.gelu(pre).astype(jnp.bfloat16)
    stream_out = (complete_input + jnp.dot(mid, point_kernel, preferred_element_type=jnp.float32)).astype(jnp.bfloat16)
    point_part = contract_rows(mid, out_grad)
    before_norm_gradient = (contract_cols(out_grad, point_kernel) * gelu_slope(pre)).astype(jnp.bfloat16)
    kernel_part = jnp.stack([contract_rows(backward_neighbor, before_norm_gradient), contract_rows(activation_value, before_norm_gradient), contract_rows(forward_neighbor, before_norm_gradient)])
    preceding_gradient = jnp.roll(before_norm_gradient, DILATION_STEP, axis=0)
    following_gradient = jnp.roll(before_norm_gradient, -DILATION_STEP, axis=0)
    act_grad = contract_cols(before_norm_gradient, conv_kernel[1])
    act_grad = act_grad + contract_cols(preceding_gradient, conv_kernel[2])
    act_grad = act_grad + contract_cols(following_gradient, conv_kernel[0])
    normalized_gradient = act_grad * gelu_slope(normalized_input)
    gain_portion = lax.optimization_barrier(jnp.sum(normalized_gradient * unit_norm_input, axis=0))
    unit_norm_gradient = normalized_gradient * norm_gain_vector
    backward_shifted = (unit_norm_gradient - unit_norm_input * lax.optimization_barrier(jnp.mean(unit_norm_gradient * unit_norm_input, axis=-1, keepdims=True))) / root_mean_square
    stream_grad = (out_grad.astype(jnp.float32) + backward_shifted).astype(jnp.bfloat16)
    carry = (carry[0] + kernel_part, carry[1] + point_part, carry[2] + gain_portion, norm_gain_vector, conv_kernel, point_kernel)
    return (carry, (stream_out, stream_grad))

def reference(stream, norm_gain_vector, conv_kernel, point_kernel, out_grad):
    start = (jnp.zeros((TAPS, C, H), jnp.float32), jnp.zeros((H, C), jnp.float32), jnp.zeros((C,), jnp.float32), norm_gain_vector, conv_kernel, point_kernel)
    carry, outs = lax.scan(one_sample, start, (stream, out_grad))
    return (outs[0], outs[1], carry[0], carry[1], carry[2])
```

```python
import jax
import jax.numpy as jnp
from jax import lax
from jax.sharding import Mesh, PartitionSpec as P

F32 = jnp.float32
BF16 = jnp.bfloat16
CHIP = ("xh", "y", "z", "xl")


def gelu_slope(value):
    return jax.jvp(jax.nn.gelu, (value,), (jnp.ones_like(value),))[1]


def dot(left, right):
    return jnp.dot(left, right, preferred_element_type=F32)


def contract_rows(left, right):
    return lax.dot_general(
        left, right, (((0,), (0,)), ((), ())), preferred_element_type=F32
    )


def contract_cols(left, right):
    return lax.dot_general(
        left, right, (((1,), (1,)), ((), ())), preferred_element_type=F32
    )


def shifted(value, by):
    axes = ("xh", "y", "z")
    return lax.ppermute(value, axes, [(i, (i + by) % 32) for i in range(32)])


def core_sum(share, core):
    half = share.shape[1] // 2
    low, high = share[:, :half], share[:, half:]
    away = jnp.where(core == 0, high, low).astype(BF16)
    kept = jnp.where(core == 0, low, high)
    return kept + lax.ppermute(away, "core", [(0, 1), (1, 0)]).astype(F32)


def shards(stream, norm_gain_vector, conv_kernel, point_kernel, out_grad):
    core = lax.axis_index("core")
    rows = stream[0].astype(F32)
    cotan = out_grad[0]
    rms = jnp.sqrt(jnp.mean(rows * rows, axis=-1, keepdims=True) + 1e-06)
    xhat = rows / rms
    normed = xhat * norm_gain_vector
    act = jax.nn.gelu(normed).astype(BF16)
    from_before = shifted(dot(act, conv_kernel[0]).astype(BF16), 8)
    from_after = shifted(dot(act, conv_kernel[2]).astype(BF16), -8)
    pre = dot(act, conv_kernel[1]) + from_before.astype(F32) + from_after.astype(F32)
    mid = jax.nn.gelu(pre).astype(BF16)
    stream_out = (rows + dot(mid, point_kernel)).astype(BF16)
    pre_grad = (contract_cols(cotan, point_kernel) * gelu_slope(pre)).astype(BF16)
    grad_before = shifted(pre_grad, 8)
    grad_after = shifted(pre_grad, -8)
    shares = [
        contract_rows(act, grad_after),
        contract_rows(act, pre_grad),
        contract_rows(act, grad_before),
        contract_rows(cotan, mid),
    ]
    act_grad = contract_cols(pre_grad, conv_kernel[1])
    act_grad = act_grad + contract_cols(grad_before, conv_kernel[2])
    act_grad = act_grad + contract_cols(grad_after, conv_kernel[0])
    norm_grad = act_grad * gelu_slope(normed)
    gain_share = jnp.sum(norm_grad * xhat, axis=0)
    hat_grad = norm_grad * norm_gain_vector
    back = (hat_grad - xhat * jnp.mean(hat_grad * xhat, axis=-1, keepdims=True)) / rms
    stream_grad = (cotan.astype(F32) + back).astype(BF16)

    parts = [core_sum(share, core).astype(BF16).reshape(32, 1, 48, 384) for share in shares]
    packed = jnp.concatenate(
        [jnp.stack([parts[0], parts[1]], 2), jnp.stack([parts[2], parts[3]], 2)], 1
    ).reshape(64, 2, 48, 384)
    got = lax.all_to_all(packed, CHIP, 0, 0, tiled=True)
    total = jnp.sum(got.astype(F32), axis=0)
    gain_got = lax.all_to_all(gain_share.reshape(128, 12), CHIP + ("core",), 0, 0, tiled=True)
    gain_total = jnp.sum(gain_got, axis=0)
    whole = lax.all_gather(total, ("xl", "core"))
    gain_grad = lax.all_gather(gain_total, ("xl", "core"), tiled=True)
    whole = whole.reshape(2, 2, 2, 48, 384).transpose(0, 2, 3, 1, 4).reshape(4, 48, 768)
    kernel_grad = whole[:3]
    point_grad = whole[3].T
    return (stream_out[None], stream_grad[None], kernel_grad, point_grad, gain_grad)


def solution(mesh):
    fine = Mesh(mesh.devices.reshape(2, 4, 4, 2, 2), ("xh", "y", "z", "xl", "core"))
    ctx, rep = ("xh", "y", "z"), ("xl", "core")
    placed = (P(rep, ctx, None), P(), P(), P(), P(rep, ctx, None))
    return jax.shard_map(
        shards,
        mesh=fine,
        in_specs=placed,
        out_specs=(
            P(rep, ctx, None),
            P(rep, ctx, None),
            P(None, ctx, None),
            P(None, ctx),
            P(ctx),
        ),
        check_vma=False,
    )
```

```python
import jax
import jax.numpy as jnp
from jax import lax
from jax.sharding import Mesh, PartitionSpec as P

F32 = jnp.float32
BF16 = jnp.bfloat16
CHIP = ("xh", "y", "z", "xl")
PLANE = ("xh", "y", "xl")
CHUNKS = 2
WIDE = 768 // CHUNKS


def gelu_slope(value):
    return jax.jvp(jax.nn.gelu, (value,), (jnp.ones_like(value),))[1]


def dot(left, right):
    return jnp.dot(left, right, preferred_element_type=F32)


def contract_rows(left, right):
    return lax.dot_general(
        left, right, (((0,), (0,)), ((), ())), preferred_element_type=F32
    )


def contract_cols(left, right):
    return lax.dot_general(
        left, right, (((1,), (1,)), ((), ())), preferred_element_type=F32
    )


def swap_x(value):
    return lax.ppermute(value, "xh", [(0, 1), (1, 0)])


def swap_y(value):
    return lax.ppermute(value, "y", [(0, 2), (1, 3), (2, 0), (3, 1)])


def swap_core(value):
    return lax.ppermute(value, "core", [(0, 1), (1, 0)])


def core_sum(first, second, takes_first):
    kept = jnp.where(takes_first, first, second)
    away = jnp.where(takes_first, second, first).astype(BF16)
    return kept + swap_core(away).astype(F32)


def shards(stream, norm_gain_vector, conv_kernel, point_kernel, out_grad):
    core = lax.axis_index("core")
    odd = lax.axis_index("y") // 2
    rows = stream[0].astype(F32)
    cotan = out_grad[0]
    rms = jnp.sqrt(jnp.mean(rows * rows, axis=-1, keepdims=True) + 1e-06)
    xhat = rows / rms
    normed = xhat * norm_gain_vector
    act = jax.nn.gelu(normed).astype(BF16)
    near = lax.dynamic_index_in_dim(conv_kernel, 2 * odd, 0, False)
    far = lax.dynamic_index_in_dim(conv_kernel, 2 - 2 * odd, 0, False)
    cut = [slice(c * WIDE, (c + 1) * WIDE) for c in range(CHUNKS)]

    crossed = [swap_x(dot(act, far[:, at]).astype(BF16)) for at in cut]
    summed = [
        swap_y((dot(act, near[:, at]) + got.astype(F32)).astype(BF16))
        for at, got in zip(cut, crossed)
    ]
    pre = [dot(act, conv_kernel[1][:, at]) + got.astype(F32) for at, got in zip(cut, summed)]
    mid = [jax.nn.gelu(value).astype(BF16) for value in pre]
    pre_grad = [
        (contract_cols(cotan, point_kernel[at]) * gelu_slope(value)).astype(BF16)
        for at, value in zip(cut, pre)
    ]
    grad_near = [swap_y(value) for value in pre_grad]
    grad_far = [swap_x(value) for value in grad_near]

    early = []
    for c in range(CHUNKS):
        share = core_sum(
            contract_rows(act, pre_grad[c]), contract_rows(cotan, mid[c]), core == 0
        ).astype(BF16)
        share = share.reshape(8, 4, 48, WIDE).transpose(1, 0, 2, 3)
        got = lax.all_to_all(share, ("z",), 0, 0, tiled=True)
        early.append(jnp.sum(got.astype(F32), axis=0).astype(BF16))
    early = jnp.stack(early, 1).reshape(16, 48, WIDE)
    early = lax.all_to_all(early, PLANE, 0, 0, tiled=True)
    early = jnp.sum(early.astype(F32), axis=0)

    stream_out = rows
    act_grad = None
    for c, at in enumerate(cut):
        stream_out = stream_out + dot(mid[c], point_kernel[at])
    stream_out = stream_out.astype(BF16)
    act_grad = contract_cols(jnp.concatenate(pre_grad, 1), conv_kernel[1])
    act_grad = act_grad + contract_cols(jnp.concatenate(grad_near, 1), near)
    act_grad = act_grad + contract_cols(jnp.concatenate(grad_far, 1), far)
    norm_grad = act_grad * gelu_slope(normed)
    gain_share = jnp.sum(norm_grad * xhat, axis=0)
    hat_grad = norm_grad * norm_gain_vector
    back = (hat_grad - xhat * jnp.mean(hat_grad * xhat, axis=-1, keepdims=True)) / rms
    stream_grad = (cotan.astype(F32) + back).astype(BF16)

    late = [
        core_sum(
            contract_rows(act, grad_near[c]), contract_rows(act, grad_far[c]), core == odd
        ).astype(BF16).reshape(32, 48, WIDE // 128, 128).transpose(0, 2, 1, 3).reshape(32, -1, 128)
        for c in range(CHUNKS)
    ]
    late = jnp.stack(late, 1).reshape(64, -1, 128)
    depth = late.shape[1]
    gain = gain_share + swap_core(gain_share)
    gain = jnp.pad(gain.astype(BF16).reshape(64, 1, 24), ((0, 0), (0, 15), (0, 104)))
    late = lax.all_to_all(jnp.concatenate([late, gain], 1), CHIP, 0, 0, tiled=True)
    late = jnp.sum(late.astype(F32), axis=0)
    gain = jnp.pad(late[depth:depth + 1, :24].reshape(24), (0, 104)).reshape(1, 128)
    late = late[:depth]
    early = early.reshape(48, WIDE // 128, 128).transpose(1, 0, 2).reshape(depth, 128)
    mine = jnp.concatenate([early, late, jnp.pad(gain, ((0, 7), (0, 0)))], 0)
    whole = lax.all_gather(mine, ("xl", "core"))

    def matrix(part):
        part = part.reshape(2, 2, WIDE // 128, 48, 128).transpose(1, 3, 0, 2, 4)
        return part.reshape(2, 48, 768)

    middle, point = matrix(whole[:, :depth])
    before, after = matrix(whole[:, depth:2 * depth])
    gain_grad = whole.reshape(2, 2, -1, 128)[:, 0, 2 * depth, :24].reshape(48)
    kernel_grad = jnp.stack([before, middle, after])
    return (stream_out[None], stream_grad[None], kernel_grad, point.T, gain_grad)


def solution(mesh):
    fine = Mesh(mesh.devices.reshape(2, 4, 4, 2, 2), ("xh", "y", "z", "xl", "core"))
    ctx, rep = ("xh", "y", "z"), ("xl", "core")
    placed = (P(rep, ctx, None), P(), P(), P(), P(rep, ctx, None))
    return jax.shard_map(
        shards,
        mesh=fine,
        in_specs=placed,
        out_specs=(
            P(rep, ctx, None),
            P(rep, ctx, None),
            P(None, ctx, None),
            P(None, ctx),
            P(ctx),
        ),
        check_vma=False,
    )
```

```python
import functools

import jax
import jax.numpy as jnp
from jax import lax
from jax.experimental import pallas as pl
from jax.experimental.pallas import tpu as pltpu
from jax.sharding import Mesh, PartitionSpec as P

F32 = jnp.float32
BF16 = jnp.bfloat16
PLANE = ("xh", "yh", "yl", "xl")
GROUP = ("xh", "yh")
Q = 128
N = 512
C = 1536
H = 768
HALF = 384
SMEM = pl.BlockSpec(memory_space=pltpu.SMEM)
ANY = pl.BlockSpec(memory_space=pl.ANY)
VMEM = pl.BlockSpec(memory_space=pltpu.VMEM)


def dot(left, right):
    return jnp.dot(left, right, preferred_element_type=F32)


def contract_cols(left, right):
    return lax.dot_general(
        left, right, (((1,), (1,)), ((), ())), preferred_element_type=F32
    )


def gelu_both(value):
    line = 0.7978845608028654 * value
    bent = line * (1.0 + 0.044715 * (value * value))
    tanh = jnp.tanh(bent)
    half = 0.5 + 0.5 * tanh
    return value * half, half + (1.0 - tanh * tanh) * (1.5 * bent - line)


def params(mebibytes):
    return pltpu.CompilerParams(vmem_limit_bytes=mebibytes * 1024 * 1024)


def cost(flops, size):
    return pl.CostEstimate(flops=flops, bytes_accessed=size, transcendentals=0)


def taps_in(odd_ref, weights_ref, held, sems):
    odd = odd_ref[0]
    return [
        pltpu.make_async_copy(weights_ref.at[tap], held.at[i], sems.at[i])
        for i, tap in enumerate((2 * odd, 1, 2 - 2 * odd))
    ]


def pack_kernel(
    me_ref, stream_ref, cotan_ref, point_ref, p0, p1, p2, p3, turned_ref,
    rows_in, turned, point, grads, in_sems, point_sem, out_sems,
):
    me = me_ref[0]
    weights = pltpu.make_async_copy(point_ref, point, point_sem)
    cotans, streams = [], []
    for k in range(4):
        rows = pl.ds(pl.multiple_of(lax.bitwise_xor(me, k) * Q, Q), Q)
        at = pl.ds(k * Q, Q)
        cotans.append(pltpu.make_async_copy(cotan_ref.at[rows], turned.at[at], in_sems.at[k]))
        streams.append(pltpu.make_async_copy(stream_ref.at[rows], rows_in.at[at], in_sems.at[4 + k]))
    for copy in cotans + [weights] + streams:
        copy.start()
    for copy in cotans:
        copy.wait()
    outs = [pltpu.make_async_copy(turned, turned_ref, out_sems.at[8])]
    outs[0].start()
    weights.wait()
    grads[...] = contract_cols(turned[...], point[...]).astype(BF16)
    for k, out in enumerate((p0, p1, p2, p3)):
        at = pl.ds(k * Q, Q)
        streams[k].wait()
        outs.append(pltpu.make_async_copy(rows_in.at[at], out.at[:, pl.ds(0, C)], out_sems.at[k]))
        outs.append(pltpu.make_async_copy(grads.at[at], out.at[:, pl.ds(C, H)], out_sems.at[4 + k]))
    for copy in outs[1:]:
        copy.start()
    for copy in outs:
        copy.wait()


def pack(me, stream, cotan, point_kernel):
    shape = jax.ShapeDtypeStruct
    return pl.pallas_call(
        pack_kernel,
        in_specs=[SMEM] + [ANY] * 3,
        out_specs=[ANY] * 5,
        out_shape=[shape((Q, C + H), BF16)] * 4 + [shape((N, C), BF16)],
        scratch_shapes=[
            pltpu.VMEM((N, C), BF16),
            pltpu.VMEM((N, C), BF16),
            pltpu.VMEM((H, C), BF16),
            pltpu.VMEM((N, H), BF16),
            pltpu.SemaphoreType.DMA((8,)),
            pltpu.SemaphoreType.DMA,
            pltpu.SemaphoreType.DMA((9,)),
        ],
        compiler_params=params(56),
        cost_estimate=cost(2 * N * C * H, 8_000_000),
        name="pack",
    )(me, stream, cotan, point_kernel)


def forward_kernel(
    odd_ref, core_ref, p0, p1, p2, p3, gain_ref, weights_ref,
    act_out, slope_out, inv_out, m0, m1, m2, m3, all_ref, kept_ref, away_ref,
    packed, ring, held, slope_in, inv_in, sems, in_sems, out_sems,
):
    ins = [
        pltpu.make_async_copy(source, packed.at[k], in_sems.at[k])
        for k, source in enumerate((p0, p1, p2, p3))
    ]
    copies = taps_in(odd_ref, weights_ref, held, sems)
    for copy in ins + copies:
        copy.start()
    core = core_ref[0]
    step = 32
    for k in range(4):
        ins[k].wait()

        def some(i, carry, k=k):
            at = pl.ds(pl.multiple_of(i * step, step), step)
            rows = packed[k, at, :C].astype(F32)
            inv = lax.rsqrt(jnp.mean(rows * rows, axis=-1, keepdims=True) + 1e-06)
            act, slope = gelu_both(rows * inv * gain_ref[...])
            here = pl.ds(pl.multiple_of(k * Q + i * step, step), step)
            slope_in[here, :] = slope
            inv_in[here, :] = jnp.broadcast_to(inv, (step, 128))
            ring[pl.ds(pl.multiple_of((k + 1) * Q + i * step, step), step), :] = act.astype(BF16)
            return carry

        lax.fori_loop(0, Q // step, some, 0)
    outs = [
        pltpu.make_async_copy(ring.at[pl.ds(Q, N)], act_out, out_sems.at[0]),
        pltpu.make_async_copy(slope_in, slope_out, out_sems.at[1]),
        pltpu.make_async_copy(inv_in, inv_out, out_sems.at[2]),
    ]
    for copy in outs:
        copy.start()
    ring[:Q] = ring[4 * Q:5 * Q]
    ring[5 * Q:] = ring[Q:2 * Q]
    for copy in copies:
        copy.wait()
    for n in range(3):
        cols = slice(n * 256, (n + 1) * 256)
        pre = dot(ring[Q:5 * Q], held[1, :, cols])
        pre = pre + dot(ring[:4 * Q], held[0, :, cols])
        pre = pre + dot(ring[2 * Q:], held[2, :, cols])
        mid, slope = gelu_both(pre)
        for k, out in enumerate((m0, m1, m2, m3)):
            at = slice(k * Q, (k + 1) * Q)
            out[:, cols] = mid[at].astype(BF16)
            grad = packed[k, :, C + n * 256:C + n * 256 + 256].astype(F32)
            all_ref[at, cols] = (grad * slope[at]).astype(BF16)
    low, high = all_ref[:, :HALF], all_ref[:, HALF:]
    kept_ref[...] = jnp.where(core == 0, low, high)
    away_ref[...] = jnp.where(core == 0, high, low)
    for copy in outs:
        copy.wait()


def forward(odd, core, pieces, gain, weights):
    shape = jax.ShapeDtypeStruct
    return pl.pallas_call(
        forward_kernel,
        in_specs=[SMEM] * 2 + [ANY] * 4 + [VMEM, ANY],
        out_specs=[ANY] * 3 + [VMEM] * 7,
        out_shape=[shape((N, C), BF16), shape((N, C), F32), shape((N, 128), F32)]
        + [shape((Q, H), BF16)] * 4
        + [shape((N, H), BF16), shape((N, HALF), BF16), shape((N, HALF), BF16)],
        scratch_shapes=[
            pltpu.VMEM((4, Q, C + H), BF16),
            pltpu.VMEM((6 * Q, C), BF16),
            pltpu.VMEM((3, C, H), BF16),
            pltpu.VMEM((N, C), F32),
            pltpu.VMEM((N, 128), F32),
            pltpu.SemaphoreType.DMA((3,)),
            pltpu.SemaphoreType.DMA((4,)),
            pltpu.SemaphoreType.DMA((3,)),
        ],
        compiler_params=params(56),
        cost_estimate=cost(6 * N * C * H, 20_000_000),
        name="forward",
    )(odd, core, *pieces, gain, weights)


def backward_kernel(
    odd_ref, grad_ref, p0, p1, p2, p3, gain_ref, slope_hbm, inv_hbm, weights_ref,
    b0, b1, b2, b3, share_ref,
    ring, held, total, slope_ref, inv_ref, rows_in, sems, in_sems,
):
    copies = taps_in(odd_ref, weights_ref, held, sems)
    copies = [copies[1], copies[0], copies[2]]
    for copy in copies:
        copy.start()
    ins = [
        pltpu.make_async_copy(slope_hbm, slope_ref, in_sems.at[0]),
        pltpu.make_async_copy(inv_hbm, inv_ref, in_sems.at[1]),
    ] + [
        pltpu.make_async_copy(source.at[:, pl.ds(0, C)], rows_in.at[k], in_sems.at[2 + k])
        for k, source in enumerate((p0, p1, p2, p3))
    ]
    for copy in ins:
        copy.start()
    ring[Q:5 * Q] = grad_ref[...]
    ring[:Q] = grad_ref[3 * Q:]
    ring[5 * Q:] = grad_ref[:Q]
    for i, copy in enumerate(copies):
        copy.wait()
        tap = (1, 0, 2)[i]
        first = (1, 2, 0)[i] * Q
        for n in range(6):
            cols = slice(n * 256, (n + 1) * 256)
            value = contract_cols(ring[first:first + N], held[tap, cols])
            total[:, cols] = value if i == 0 else total[:, cols] + value
    for copy in ins:
        copy.wait()
    step = 32
    share = jnp.zeros((8, C), F32)
    for k, out in enumerate((b0, b1, b2, b3)):

        def some(i, share, k=k, out=out):
            at = pl.ds(pl.multiple_of(i * step, step), step)
            here = pl.ds(pl.multiple_of(k * Q + i * step, step), step)
            inv = inv_ref[here, :1]
            hat = rows_in[k, at, :].astype(F32) * inv
            norm_grad = total[here, :] * slope_ref[here, :]
            product = norm_grad * hat
            mean = jnp.mean(product * gain_ref[...], axis=-1, keepdims=True)
            out[at, :] = ((norm_grad * gain_ref[...] - hat * mean) * inv).astype(BF16)
            return share + product.reshape(step // 8, 8, C).sum(0)

        share = lax.fori_loop(0, Q // step, some, share)
    share_ref[...] = jnp.sum(share, axis=0, keepdims=True)


def backward(odd, grads, pieces, gain, slope, inv, weights):
    shape = jax.ShapeDtypeStruct
    return pl.pallas_call(
        backward_kernel,
        in_specs=[SMEM, VMEM] + [ANY] * 4 + [VMEM] + [ANY] * 3,
        out_specs=[VMEM] * 5,
        out_shape=[shape((Q, C), BF16)] * 4 + [shape((1, C), F32)],
        scratch_shapes=[
            pltpu.VMEM((6 * Q, H), BF16),
            pltpu.VMEM((3, C, H), BF16),
            pltpu.VMEM((N, C), F32),
            pltpu.VMEM((N, C), F32),
            pltpu.VMEM((N, 128), F32),
            pltpu.VMEM((4, Q, C), BF16),
            pltpu.SemaphoreType.DMA((3,)),
            pltpu.SemaphoreType.DMA((6,)),
        ],
        compiler_params=params(56),
        cost_estimate=cost(6 * N * C * H, 20_000_000),
        name="backward",
    )(odd, grads, *pieces, gain, slope, inv, weights)


def kernel_share_kernel(odd_ref, own_ref, other_ref, kept_ref, came_ref, out_ref, right, ring):
    @pl.when(pl.program_id(0) == 0)
    def _():
        odd = odd_ref[0]
        for i, source in enumerate((kept_ref, came_ref)):
            ring[Q:5 * Q] = source[...]
            ring[:Q] = source[3 * Q:]
            ring[5 * Q:] = source[:Q]
            rows = slice(i * N, (i + 1) * N)
            near = pl.multiple_of(jnp.where(odd == 0, 2 * Q, 0), Q)
            far = pl.multiple_of(jnp.where(odd == 0, 0, 2 * Q), Q)
            right[rows, :HALF] = ring[pl.ds(near, N), :]
            right[rows, HALF:2 * HALF] = source[...]
            right[rows, 2 * HALF:] = ring[pl.ds(far, N), :]

    value = dot(own_ref[...], right[:N]) + dot(other_ref[...], right[N:])
    value = value.astype(BF16)
    for t in range(3):
        for b in range(3):
            at = t * HALF + b * 128
            part = value[:, at:at + 128].reshape(2, 4, 48, 128)
            for z in range(4):
                out_ref[z, :, t, 48 * b:48 * b + 48, :] = part[:, z]


def kernel_shares(odd, own, other, kept, came):
    whole = pl.BlockSpec((N, HALF), lambda i: (0, 0))
    part = pl.BlockSpec((C // 4, N), lambda i: (i, 0))
    return pl.pallas_call(
        kernel_share_kernel,
        grid=(4,),
        in_specs=[SMEM, part, part, whole, whole],
        out_specs=pl.BlockSpec((4, 2, 3, 144, 128), lambda i: (0, i, 0, 0, 0)),
        out_shape=jax.ShapeDtypeStruct((4, 8, 3, 144, 128), BF16),
        scratch_shapes=[pltpu.VMEM((2 * N, 3 * HALF), BF16), pltpu.VMEM((6 * Q, HALF), BF16)],
        compiler_params=params(56),
        cost_estimate=cost(6 * N * C * H, 10_000_000),
        name="kernel_shares",
    )(odd, own, other, kept, came)


def point_share_kernel(own_ref, other_ref, kept_ref, came_ref, gain_ref, out_ref):
    out_ref[:, :, 144:, :] = gain_ref[...]
    value = dot(own_ref[...], kept_ref[...]) + dot(other_ref[...], came_ref[...])
    value = value.astype(BF16)
    for b in range(3):
        part = value[:, b * 128:b * 128 + 128].reshape(2, 4, 48, 128)
        for z in range(4):
            out_ref[z, :, 48 * b:48 * b + 48, :] = part[:, z]


def point_shares(own, other, kept, came, gain):
    whole = pl.BlockSpec((N, HALF), lambda i: (0, 0))
    part = pl.BlockSpec((C // 4, N), lambda i: (i, 0))
    return pl.pallas_call(
        point_share_kernel,
        grid=(4,),
        in_specs=[part, part, whole, whole, pl.BlockSpec((4, 2, 16, 128), lambda i: (0, i, 0, 0))],
        out_specs=pl.BlockSpec((4, 2, 160, 128), lambda i: (0, i, 0, 0)),
        out_shape=jax.ShapeDtypeStruct((4, 8, 160, 128), BF16),
        compiler_params=params(56),
        cost_estimate=cost(2 * N * C * H, 6_000_000),
        name="point_shares",
    )(own, other, kept, came, gain)


def swap_core(value):
    return lax.ppermute(value, "core", [(0, 1), (1, 0)])


def exchange(pieces):
    return [pieces[0]] + [
        lax.ppermute(pieces[k], GROUP, [(i, i ^ k) for i in range(4)]) for k in (1, 2, 3)
    ]


def restored(pieces, me):
    pairs = []
    for a, b in (pieces[:2], pieces[2:]):
        turn = (me & 1) == 1
        pairs.append(jnp.stack([jnp.where(turn, b, a), jnp.where(turn, a, b)]))
    low, high = pairs
    turn = (me & 2) == 2
    out = jnp.concatenate([jnp.where(turn, high, low), jnp.where(turn, low, high)])
    return out.reshape(N, out.shape[2])


def shards(stream, norm_gain_vector, conv_kernel, point_kernel, out_grad):
    core = lax.axis_index("core").astype(jnp.int32)
    odd = lax.axis_index("yh").astype(jnp.int32)
    me = 2 * lax.axis_index("xh") + odd
    core_word, odd_word = core.reshape(1), odd.reshape(1)
    gain_row = norm_gain_vector.reshape(1, C)
    cotan = out_grad[0]

    packed = pack(me.reshape(1), stream[0], cotan, point_kernel)
    pieces = exchange(packed[:4])
    cotan_cols = packed[4].T
    cotan_other = swap_core(cotan_cols)

    act, slope_in, inv, m0, m1, m2, m3, pre_grad, kept, away = forward(
        odd_word, core_word, pieces, gain_row, conv_kernel
    )
    act_cols = act.T
    act_other = swap_core(act_cols)
    came = swap_core(away)
    shares = kernel_shares(odd_word, act_cols, act_other, kept, came)
    shares, pre_grad, *mid = lax.optimization_barrier((shares, pre_grad, m0, m1, m2, m3))
    shares = lax.all_to_all(shares, "z", 0, 0, tiled=True)
    mid = exchange(mid)
    b0, b1, b2, b3, gain = backward(
        odd_word, pre_grad, pieces, gain_row, slope_in, inv, conv_kernel
    )
    gain, *mid = lax.optimization_barrier((gain, *mid))
    back = exchange([b0, b1, b2, b3])

    mid = jnp.concatenate(mid)
    low, high = mid[:, :HALF], mid[:, HALF:]
    mid_kept = jnp.where(core == 0, low, high)
    mid_came = swap_core(jnp.where(core == 0, high, low))
    gain = gain.astype(BF16).reshape(8, 4, 1, 48).transpose(1, 0, 2, 3)
    gain = jnp.pad(gain, ((0, 0), (0, 0), (0, 15), (0, 80)))
    point_part = point_shares(cotan_cols, cotan_other, mid_kept, mid_came, gain)
    shares, point_part = lax.optimization_barrier((shares, point_part))
    point_part = lax.all_to_all(point_part, "z", 0, 0, tiled=True)
    shares = jnp.sum(shares.astype(F32), axis=0).astype(BF16)
    point_part = jnp.sum(point_part.astype(F32), axis=0).astype(BF16)
    first = [shares[:, 0], shares[:, 1], point_part[:, 144:]]
    second = [shares[:, 2], point_part]
    plane = jnp.stack([jnp.concatenate(first, 1), jnp.concatenate(second, 1)], 1)
    plane, *back = lax.optimization_barrier((plane, *back))
    got = lax.all_to_all(plane.reshape(16, 304, 128), PLANE, 0, 0, tiled=True)

    stream_out = dot(mid, point_kernel).reshape(4, Q, C)
    stream_out = restored([stream_out[k] for k in range(4)], me)
    stream_out = (stream[0].astype(F32) + stream_out).astype(BF16)
    stream_grad = (cotan.astype(F32) + restored(back, me).astype(F32)).astype(BF16)

    total = jnp.sum(got.astype(F32), axis=0)[:296]
    whole = lax.all_gather(total, ("xl", "core"))
    gain_grad = whole[0, 288, :48] + whole[1, 288, :48]
    whole = whole[:, :288].reshape(2, 2, 2, 3, 48, 128).transpose(0, 2, 4, 1, 3, 5)
    whole = whole.reshape(4, 48, H)
    kernel_grad = jnp.stack([whole[0], whole[1], whole[2]])
    return (stream_out[None], stream_grad[None], kernel_grad, whole[3].T, gain_grad)


def solution(mesh):
    fine = Mesh(
        mesh.devices.reshape(2, 2, 2, 4, 2, 2), ("xh", "yh", "yl", "z", "xl", "core")
    )
    ctx, rep = ("xh", "yh", "yl", "z"), ("xl", "core")
    placed = (P(rep, ctx, None), P(), P(), P(), P(rep, ctx, None))
    return jax.shard_map(
        shards,
        mesh=fine,
        in_specs=placed,
        out_specs=(
            P(rep, ctx, None),
            P(rep, ctx, None),
            P(None, ctx, None),
            P(None, ctx),
            P(ctx),
        ),
        check_vma=False,
    )
```

```python
import functools

import jax
import jax.numpy as jnp
from jax import lax
from jax.experimental import pallas as pl
from jax.experimental.pallas import tpu as pltpu
from jax.sharding import Mesh, PartitionSpec as P

F32 = jnp.float32
BF16 = jnp.bfloat16
PLANE = ("xh", "yh", "yl", "xl")
GROUP = ("xh", "yh")
Q = 128
N = 512
C = 1536
H = 768
HALF = 384
SMEM = pl.BlockSpec(memory_space=pltpu.SMEM)
ANY = pl.BlockSpec(memory_space=pl.ANY)
VMEM = pl.BlockSpec(memory_space=pltpu.VMEM)


def dot(left, right):
    return jnp.dot(left, right, preferred_element_type=F32)


def contract_rows(left, right):
    return lax.dot_general(
        left, right, (((0,), (0,)), ((), ())), preferred_element_type=F32
    )


def contract_cols(left, right):
    return lax.dot_general(
        left, right, (((1,), (1,)), ((), ())), preferred_element_type=F32
    )


def gelu_both(value):
    line = 0.7978845608028654 * value
    bent = line * (1.0 + 0.044715 * (value * value))
    tanh = jnp.tanh(bent)
    half = 0.5 + 0.5 * tanh
    return value * half, half + (1.0 - tanh * tanh) * (1.5 * bent - line)


def params(mebibytes):
    return pltpu.CompilerParams(vmem_limit_bytes=mebibytes * 1024 * 1024)


def cost(flops, size):
    return pl.CostEstimate(flops=flops, bytes_accessed=size, transcendentals=0)


def taps_in(odd_ref, weights_ref, held, sems):
    odd = odd_ref[0]
    return [
        pltpu.make_async_copy(weights_ref.at[tap], held.at[i], sems.at[i])
        for i, tap in enumerate((2 * odd, 1, 2 - 2 * odd))
    ]


def pack_kernel(
    me_ref, stream_ref, cotan_ref, point_ref, p0, p1, p2, p3, turned_ref,
    rows_in, turned, point, grads, in_sems, point_sem, out_sems,
):
    me = me_ref[0]
    weights = pltpu.make_async_copy(point_ref, point, point_sem)
    cotans, streams = [], []
    for k in range(4):
        rows = pl.ds(pl.multiple_of(lax.bitwise_xor(me, k) * Q, Q), Q)
        at = pl.ds(k * Q, Q)
        cotans.append(pltpu.make_async_copy(cotan_ref.at[rows], turned.at[at], in_sems.at[k]))
        streams.append(pltpu.make_async_copy(stream_ref.at[rows], rows_in.at[at], in_sems.at[4 + k]))
    for copy in cotans + [weights] + streams:
        copy.start()
    for copy in cotans:
        copy.wait()
    outs = [pltpu.make_async_copy(turned, turned_ref, out_sems.at[8])]
    outs[0].start()
    weights.wait()
    grads[...] = contract_cols(turned[...], point[...]).astype(BF16)
    for k, out in enumerate((p0, p1, p2, p3)):
        at = pl.ds(k * Q, Q)
        streams[k].wait()
        outs.append(pltpu.make_async_copy(rows_in.at[at], out.at[:, pl.ds(0, C)], out_sems.at[k]))
        outs.append(pltpu.make_async_copy(grads.at[at], out.at[:, pl.ds(C, H)], out_sems.at[4 + k]))
    for copy in outs[1:]:
        copy.start()
    for copy in outs:
        copy.wait()


def pack(me, stream, cotan, point_kernel):
    shape = jax.ShapeDtypeStruct
    return pl.pallas_call(
        pack_kernel,
        in_specs=[SMEM] + [ANY] * 3,
        out_specs=[ANY] * 5,
        out_shape=[shape((Q, C + H), BF16)] * 4 + [shape((N, C), BF16)],
        scratch_shapes=[
            pltpu.VMEM((N, C), BF16),
            pltpu.VMEM((N, C), BF16),
            pltpu.VMEM((H, C), BF16),
            pltpu.VMEM((N, H), BF16),
            pltpu.SemaphoreType.DMA((8,)),
            pltpu.SemaphoreType.DMA,
            pltpu.SemaphoreType.DMA((9,)),
        ],
        compiler_params=params(56),
        cost_estimate=cost(2 * N * C * H, 8_000_000),
        name="pack",
    )(me, stream, cotan, point_kernel)


def forward_kernel(
    odd_ref, core_ref, p0, p1, p2, p3, gain_ref, weights_ref,
    act_out, slope_out, inv_out, m0, m1, m2, m3, all_ref, kept_ref, away_ref,
    packed, ring, held, slope_in, inv_in, sems, in_sems, out_sems,
):
    ins = [
        pltpu.make_async_copy(source, packed.at[k], in_sems.at[k])
        for k, source in enumerate((p0, p1, p2, p3))
    ]
    copies = taps_in(odd_ref, weights_ref, held, sems)
    for copy in ins + copies:
        copy.start()
    core = core_ref[0]
    step = 64
    for k in range(4):
        ins[k].wait()

        def some(i, carry, k=k):
            at = pl.ds(pl.multiple_of(i * step, step), step)
            rows = packed[k, at, :C].astype(F32)
            inv = lax.rsqrt(jnp.mean(rows * rows, axis=-1, keepdims=True) + 1e-06)
            act, slope = gelu_both(rows * inv * gain_ref[...])
            here = pl.ds(pl.multiple_of(k * Q + i * step, step), step)
            slope_in[here, :] = slope
            inv_in[here, :] = jnp.broadcast_to(inv, (step, 128))
            ring[pl.ds(pl.multiple_of((k + 1) * Q + i * step, step), step), :] = act.astype(BF16)
            return carry

        lax.fori_loop(0, Q // step, some, 0)
    outs = [
        pltpu.make_async_copy(ring.at[pl.ds(Q, N)], act_out, out_sems.at[0]),
        pltpu.make_async_copy(slope_in, slope_out, out_sems.at[1]),
        pltpu.make_async_copy(inv_in, inv_out, out_sems.at[2]),
    ]
    for copy in outs:
        copy.start()
    ring[:Q] = ring[4 * Q:5 * Q]
    ring[5 * Q:] = ring[Q:2 * Q]
    for copy in copies:
        copy.wait()
    for n in range(3):
        cols = slice(n * 256, (n + 1) * 256)
        pre = dot(ring[Q:5 * Q], held[1, :, cols])
        pre = pre + dot(ring[:4 * Q], held[0, :, cols])
        pre = pre + dot(ring[2 * Q:], held[2, :, cols])
        mid, slope = gelu_both(pre)
        for k, out in enumerate((m0, m1, m2, m3)):
            at = slice(k * Q, (k + 1) * Q)
            out[:, cols] = mid[at].astype(BF16)
            grad = packed[k, :, C + n * 256:C + n * 256 + 256].astype(F32)
            all_ref[at, cols] = (grad * slope[at]).astype(BF16)
    low, high = all_ref[:, :HALF], all_ref[:, HALF:]
    kept_ref[...] = jnp.where(core == 0, low, high)
    away_ref[...] = jnp.where(core == 0, high, low)
    for copy in outs:
        copy.wait()


def forward(odd, core, pieces, gain, weights):
    shape = jax.ShapeDtypeStruct
    return pl.pallas_call(
        forward_kernel,
        in_specs=[SMEM] * 2 + [ANY] * 4 + [VMEM, ANY],
        out_specs=[ANY] * 3 + [VMEM] * 7,
        out_shape=[shape((N, C), BF16), shape((N, C), F32), shape((N, 128), F32)]
        + [shape((Q, H), BF16)] * 4
        + [shape((N, H), BF16), shape((N, HALF), BF16), shape((N, HALF), BF16)],
        scratch_shapes=[
            pltpu.VMEM((4, Q, C + H), BF16),
            pltpu.VMEM((6 * Q, C), BF16),
            pltpu.VMEM((3, C, H), BF16),
            pltpu.VMEM((N, C), F32),
            pltpu.VMEM((N, 128), F32),
            pltpu.SemaphoreType.DMA((3,)),
            pltpu.SemaphoreType.DMA((4,)),
            pltpu.SemaphoreType.DMA((3,)),
        ],
        compiler_params=params(56),
        cost_estimate=cost(6 * N * C * H, 20_000_000),
        name="forward",
    )(odd, core, *pieces, gain, weights)


def backward_kernel(
    odd_ref, grad_ref, p0, p1, p2, p3, gain_ref, slope_hbm, inv_hbm, weights_ref,
    b0, b1, b2, b3, share_ref,
    ring, held, total, slope_ref, inv_ref, rows_in, sems, in_sems,
):
    copies = taps_in(odd_ref, weights_ref, held, sems)
    copies = [copies[1], copies[0], copies[2]]
    for copy in copies:
        copy.start()
    ins = [
        pltpu.make_async_copy(slope_hbm, slope_ref, in_sems.at[0]),
        pltpu.make_async_copy(inv_hbm, inv_ref, in_sems.at[1]),
    ] + [
        pltpu.make_async_copy(source.at[:, pl.ds(0, C)], rows_in.at[k], in_sems.at[2 + k])
        for k, source in enumerate((p0, p1, p2, p3))
    ]
    for copy in ins:
        copy.start()
    ring[Q:5 * Q] = grad_ref[...]
    ring[:Q] = grad_ref[3 * Q:]
    ring[5 * Q:] = grad_ref[:Q]
    for i, copy in enumerate(copies):
        copy.wait()
        tap = (1, 0, 2)[i]
        first = (1, 2, 0)[i] * Q
        for n in range(6):
            cols = slice(n * 256, (n + 1) * 256)
            value = contract_cols(ring[first:first + N], held[tap, cols])
            total[:, cols] = value if i == 0 else total[:, cols] + value
    for copy in ins:
        copy.wait()
    step = 64
    share = jnp.zeros((8, C), F32)
    for k, out in enumerate((b0, b1, b2, b3)):

        def some(i, share, k=k, out=out):
            at = pl.ds(pl.multiple_of(i * step, step), step)
            here = pl.ds(pl.multiple_of(k * Q + i * step, step), step)
            inv = inv_ref[here, :1]
            hat = rows_in[k, at, :].astype(F32) * inv
            norm_grad = total[here, :] * slope_ref[here, :]
            product = norm_grad * hat
            mean = jnp.mean(product * gain_ref[...], axis=-1, keepdims=True)
            out[at, :] = ((norm_grad * gain_ref[...] - hat * mean) * inv).astype(BF16)
            return share + product.reshape(step // 8, 8, C).sum(0)

        share = lax.fori_loop(0, Q // step, some, share)
    share_ref[...] = jnp.sum(share, axis=0, keepdims=True)


def backward(odd, grads, pieces, gain, slope, inv, weights):
    shape = jax.ShapeDtypeStruct
    return pl.pallas_call(
        backward_kernel,
        in_specs=[SMEM, VMEM] + [ANY] * 4 + [VMEM] + [ANY] * 3,
        out_specs=[VMEM] * 5,
        out_shape=[shape((Q, C), BF16)] * 4 + [shape((1, C), F32)],
        scratch_shapes=[
            pltpu.VMEM((6 * Q, H), BF16),
            pltpu.VMEM((3, C, H), BF16),
            pltpu.VMEM((N, C), F32),
            pltpu.VMEM((N, C), F32),
            pltpu.VMEM((N, 128), F32),
            pltpu.VMEM((4, Q, C), BF16),
            pltpu.SemaphoreType.DMA((3,)),
            pltpu.SemaphoreType.DMA((6,)),
        ],
        compiler_params=params(56),
        cost_estimate=cost(1_000_000, 100_000),
        name="backward",
    )(odd, grads, *pieces, gain, slope, inv, weights)


def load_columns(own_hbm, other_hbm, own, other, sems):
    ins = []
    for i in range(4):
        cols = pl.ds(i * HALF, HALF)
        ins.append((
            pltpu.make_async_copy(own_hbm.at[:, cols], own.at[i], sems.at[2 * i]),
            pltpu.make_async_copy(other_hbm.at[:, cols], other.at[i], sems.at[2 * i + 1]),
        ))
        for copy in ins[-1]:
            copy.start()
    return ins


def kernel_share_kernel(
    odd_ref, own_hbm, other_hbm, kept_ref, came_ref, out_ref,
    own, other, right, ring, value, in_sems, out_sems,
):
    ins = load_columns(own_hbm, other_hbm, own, other, in_sems)
    odd = odd_ref[0]
    near = pl.multiple_of(jnp.where(odd == 0, 2 * Q, 0), Q)
    far = pl.multiple_of(jnp.where(odd == 0, 0, 2 * Q), Q)
    for i, source in enumerate((kept_ref, came_ref)):
        ring[Q:5 * Q] = source[...]
        ring[:Q] = source[3 * Q:]
        ring[5 * Q:] = source[:Q]
        rows = slice(i * N, (i + 1) * N)
        right[rows, :HALF] = ring[pl.ds(near, N), :]
        right[rows, HALF:2 * HALF] = source[...]
        right[rows, 2 * HALF:] = ring[pl.ds(far, N), :]
    outs = []
    for i in range(4):
        for copy in ins[i]:
            copy.wait()
        part = contract_rows(own[i], right[:N]) + contract_rows(other[i], right[N:])
        part = part.astype(BF16)
        for b in range(9):
            value[2 * i:2 * i + 2, :, 48 * b:48 * b + 48, :] = part[
                :, 128 * b:128 * b + 128
            ].reshape(2, 4, 48, 128)
        for g in (2 * i, 2 * i + 1):
            outs.append(
                pltpu.make_async_copy(value.at[g], out_ref.at[:, g], out_sems.at[g])
            )
            outs[-1].start()
    for copy in outs:
        copy.wait()


def kernel_shares(odd, own, other, kept, came):
    return pl.pallas_call(
        kernel_share_kernel,
        in_specs=[SMEM, ANY, ANY, VMEM, VMEM],
        out_specs=ANY,
        out_shape=jax.ShapeDtypeStruct((4, 8, 432, 128), BF16),
        scratch_shapes=[
            pltpu.VMEM((4, N, HALF), BF16),
            pltpu.VMEM((4, N, HALF), BF16),
            pltpu.VMEM((2 * N, 3 * HALF), BF16),
            pltpu.VMEM((6 * Q, HALF), BF16),
            pltpu.VMEM((8, 4, 432, 128), BF16),
            pltpu.SemaphoreType.DMA((8,)),
            pltpu.SemaphoreType.DMA((8,)),
        ],
        compiler_params=params(56),
        cost_estimate=cost(6 * N * C * H, 10_000_000),
        name="kernel_shares",
    )(odd, own, other, kept, came)


def point_share_kernel(
    z_ref, own_hbm, other_hbm, kept_ref, came_ref, gain_ref, d0, d1, d2, d3,
    own, other, value, in_sems, out_sems,
):
    ins = load_columns(own_hbm, other_hbm, own, other, in_sems)
    value[:, :, 144:] = gain_ref[...]
    outs = []
    for i in range(4):
        for copy in ins[i]:
            copy.wait()
        part = contract_rows(own[i], kept_ref[...]) + contract_rows(other[i], came_ref[...])
        part = part.astype(BF16)
        for b in range(3):
            value[2 * i:2 * i + 2, :, 48 * b:48 * b + 48, :] = part[
                :, 128 * b:128 * b + 128
            ].reshape(2, 4, 48, 128)
        for g in (2 * i, 2 * i + 1):
            for d, out in enumerate((d0, d1, d2, d3)):
                source = value.at[g, lax.rem(z_ref[0] + d, 4)]
                outs.append(pltpu.make_async_copy(source, out.at[g], out_sems.at[len(outs)]))
                outs[-1].start()
    for copy in outs:
        copy.wait()


def point_shares(z, own, other, kept, came, gain):
    return pl.pallas_call(
        point_share_kernel,
        in_specs=[SMEM, ANY, ANY, VMEM, VMEM, VMEM],
        out_specs=[ANY] * 4,
        out_shape=[jax.ShapeDtypeStruct((8, 160, 128), BF16)] * 4,
        scratch_shapes=[
            pltpu.VMEM((4, N, HALF), BF16),
            pltpu.VMEM((4, N, HALF), BF16),
            pltpu.VMEM((8, 4, 160, 128), BF16),
            pltpu.SemaphoreType.DMA((8,)),
            pltpu.SemaphoreType.DMA((32,)),
        ],
        compiler_params=params(56),
        cost_estimate=cost(2 * N * C * H, 6_000_000),
        name="point_shares",
    )(z, own, other, kept, came, gain)


def four_sum(a, b, c, d):
    return ((a.astype(F32) + b.astype(F32)) + (c.astype(F32) + d.astype(F32))).astype(BF16)


def tap_sum_kernel(shares_ref, out_ref):
    out_ref[...] = four_sum(*[shares_ref[i] for i in range(4)])


def tap_sums(shares):
    return pl.pallas_call(
        tap_sum_kernel,
        grid=(4,),
        in_specs=[pl.BlockSpec((4, 2, 432, 128), lambda g: (0, g, 0, 0))],
        out_specs=pl.BlockSpec((2, 432, 128), lambda g: (g, 0, 0)),
        out_shape=jax.ShapeDtypeStruct((8, 432, 128), BF16),
        compiler_params=params(32),
        cost_estimate=cost(3_000_000, 5_000_000),
        name="tap_sums",
    )(shares)


def plane_kernel(taps_ref, d0, d1, d2, d3, out_ref):
    point = four_sum(d0[...], d1[...], d2[...], d3[...])
    out_ref[:, 0, :288] = taps_ref[:, :288]
    out_ref[:, 1, :144] = taps_ref[:, 288:]
    out_ref[:, 1, 144:288] = point[:, :144]
    for chip in range(2):
        out_ref[:, chip, 288:] = point[:, 144:]


def plane_shares(taps, points):
    return pl.pallas_call(
        plane_kernel,
        in_specs=[VMEM] * 5,
        out_specs=VMEM,
        out_shape=jax.ShapeDtypeStruct((8, 2, 304, 128), BF16),
        compiler_params=params(32),
        cost_estimate=cost(1_000_000, 3_000_000),
        name="plane_shares",
    )(taps, *points)


def home_rows(me_ref, k):
    return pl.ds(pl.multiple_of(lax.bitwise_xor(me_ref[0], k) * Q, Q), Q)


def stream_out_kernel(
    me_ref, m0, m1, m2, m3, point_ref, stream_ref, out_ref,
    mid, point, rows, result, in_sems, out_sems,
):
    ins = [pltpu.make_async_copy(point_ref, point, in_sems.at[8])]
    for k, source in enumerate((m0, m1, m2, m3)):
        at = pl.ds(k * Q, Q)
        ins.append(pltpu.make_async_copy(source, mid.at[at], in_sems.at[k]))
        ins.append(
            pltpu.make_async_copy(stream_ref.at[home_rows(me_ref, k)], rows.at[at], in_sems.at[4 + k])
        )
    for copy in ins:
        copy.start()
    for copy in ins:
        copy.wait()
    for n in range(6):
        cols = slice(n * 256, (n + 1) * 256)
        result[:, cols] = (rows[:, cols].astype(F32) + dot(mid[...], point[:, cols])).astype(BF16)
    outs = [
        pltpu.make_async_copy(
            result.at[pl.ds(k * Q, Q)], out_ref.at[home_rows(me_ref, k)], out_sems.at[k]
        )
        for k in range(4)
    ]
    for copy in outs:
        copy.start()
    for copy in outs:
        copy.wait()


def home_stream_out(me, mid, point_kernel, stream):
    return pl.pallas_call(
        stream_out_kernel,
        in_specs=[SMEM] + [ANY] * 6,
        out_specs=ANY,
        out_shape=jax.ShapeDtypeStruct((N, C), BF16),
        scratch_shapes=[
            pltpu.VMEM((N, H), BF16),
            pltpu.VMEM((H, C), BF16),
            pltpu.VMEM((N, C), BF16),
            pltpu.VMEM((N, C), BF16),
            pltpu.SemaphoreType.DMA((9,)),
            pltpu.SemaphoreType.DMA((4,)),
        ],
        compiler_params=params(56),
        cost_estimate=cost(2 * N * C * H, 6_000_000),
        name="stream_out",
    )(me, *mid, point_kernel, stream)


def stream_grad_kernel(
    me_ref, b0, b1, b2, b3, cotan_ref, out_ref, back, rows, in_sems, out_sems
):
    ins = []
    for k, source in enumerate((b0, b1, b2, b3)):
        ins.append((
            pltpu.make_async_copy(source, back.at[k], in_sems.at[k]),
            pltpu.make_async_copy(cotan_ref.at[home_rows(me_ref, k)], rows.at[k], in_sems.at[4 + k]),
        ))
        for copy in ins[-1]:
            copy.start()
    outs = []
    for k in range(4):
        for copy in ins[k]:
            copy.wait()
        rows[k] = (rows[k].astype(F32) + back[k].astype(F32)).astype(BF16)
        outs.append(
            pltpu.make_async_copy(rows.at[k], out_ref.at[home_rows(me_ref, k)], out_sems.at[k])
        )
        outs[-1].start()
    for copy in outs:
        copy.wait()


def home_stream_grad(me, back, cotan):
    return pl.pallas_call(
        stream_grad_kernel,
        in_specs=[SMEM] + [ANY] * 5,
        out_specs=ANY,
        out_shape=jax.ShapeDtypeStruct((N, C), BF16),
        scratch_shapes=[
            pltpu.VMEM((4, Q, C), BF16),
            pltpu.VMEM((4, Q, C), BF16),
            pltpu.SemaphoreType.DMA((8,)),
            pltpu.SemaphoreType.DMA((4,)),
        ],
        compiler_params=params(56),
        cost_estimate=cost(2 * N * C, 5_000_000),
        name="stream_grad",
    )(me, *back, cotan)


def swap_core(value):
    return lax.ppermute(value, "core", [(0, 1), (1, 0)])


def partner(value, k):
    return lax.ppermute(value, GROUP, [(i, i ^ k) for i in range(4)])


def exchange(pieces):
    return [pieces[0]] + [partner(pieces[k], k) for k in range(1, len(pieces))]


def shards(stream, norm_gain_vector, conv_kernel, point_kernel, out_grad):
    core = lax.axis_index("core").astype(jnp.int32)
    odd = lax.axis_index("yh").astype(jnp.int32)
    me = 2 * lax.axis_index("xh") + odd
    z = lax.axis_index("z").astype(jnp.int32)
    core_word, odd_word, z_word = core.reshape(1), odd.reshape(1), z.reshape(1)
    gain_row = norm_gain_vector.reshape(1, C)
    cotan = out_grad[0]

    packed = pack(me.reshape(1), stream[0], cotan, point_kernel)
    pieces = exchange(packed[:4])
    cotan_turned = packed[4]
    cotan_other = swap_core(cotan_turned)

    act, slope_in, inv, m0, m1, m2, m3, pre_grad, kept, away = forward(
        odd_word, core_word, pieces, gain_row, conv_kernel
    )
    act_other = swap_core(act)
    came = swap_core(away)
    shares = kernel_shares(odd_word, act, act_other, kept, came)
    shares, pre_grad, m0, m1, m2, m3 = lax.optimization_barrier(
        (shares, pre_grad, m0, m1, m2, m3)
    )
    shares = lax.all_to_all(shares, "z", 0, 0, tiled=True)
    mid = exchange([m0, m1, m2, m3])
    b0, b1, b2, b3, gain = backward(
        odd_word, pre_grad, pieces, gain_row, slope_in, inv, conv_kernel
    )
    back = exchange([b0, b1, b2, b3])
    gain, *mid = lax.optimization_barrier((gain, *mid))
    mid_home = jnp.concatenate(mid)
    low, high = mid_home[:, :HALF], mid_home[:, HALF:]
    mid_kept = jnp.where(core == 0, low, high)
    mid_came = swap_core(jnp.where(core == 0, high, low))
    gain = gain.astype(BF16).reshape(8, 4, 1, 48)
    gain = jnp.pad(gain, ((0, 0), (0, 0), (0, 15), (0, 80)))
    points = list(
        point_shares(z_word, cotan_turned, cotan_other, mid_kept, mid_came, gain)
    )
    points[0], points[1], points[2], points[3], back[1], back[2], *mid = lax.optimization_barrier(
        (*points, back[1], back[2], *mid)
    )
    points = [points[0]] + [
        lax.ppermute(points[d], "z", [(i, (i + d) % 4) for i in range(4)]) for d in (1, 2, 3)
    ]
    stream_out = home_stream_out(me.reshape(1), mid, point_kernel, stream[0])
    shares, stream_out = lax.optimization_barrier((shares, stream_out))
    taps = tap_sums(shares)
    stream_grad = home_stream_grad(me.reshape(1), back, cotan)
    taps, stream_grad, *points = lax.optimization_barrier((taps, stream_grad, *points))
    plane = plane_shares(taps, points).reshape(16, 304, 128)
    plane = lax.all_to_all(plane, PLANE, 0, 0, tiled=True)
    plane = jnp.sum(plane.astype(F32), axis=0)[:296]
    whole = lax.all_gather(plane, ("xl", "core"))
    gain_grad = whole[0, 288, :48] + whole[1, 288, :48]
    whole = whole[:, :288].reshape(2, 2, 2, 3, 48, 128).transpose(0, 2, 4, 1, 3, 5)
    whole = whole.reshape(4, 48, H)
    kernel_grad = jnp.stack([whole[0], whole[1], whole[2]])
    return (stream_out[None], stream_grad[None], kernel_grad, whole[3].T, gain_grad)


def solution(mesh):
    fine = Mesh(
        mesh.devices.reshape(2, 2, 2, 4, 2, 2), ("xh", "yh", "yl", "z", "xl", "core")
    )
    ctx, rep = ("xh", "yh", "yl", "z"), ("xl", "core")
    placed = (P(rep, ctx, None), P(), P(), P(), P(rep, ctx, None))
    return jax.shard_map(
        shards,
        mesh=fine,
        in_specs=placed,
        out_specs=(
            P(rep, ctx, None),
            P(rep, ctx, None),
            P(None, ctx, None),
            P(None, ctx),
            P(ctx),
        ),
        check_vma=False,
    )
```

```python
import functools

import jax
import jax.numpy as jnp
from jax import lax
from jax.experimental import pallas as pl
from jax.experimental.pallas import tpu as pltpu
from jax.sharding import Mesh, PartitionSpec as P

F32 = jnp.float32
BF16 = jnp.bfloat16
PLANE = ("xh", "yh", "yl", "xl")
GROUP = ("xh", "yh")
Q = 128
N = 512
C = 1536
H = 768
HALF = 384
SMEM = pl.BlockSpec(memory_space=pltpu.SMEM)
ANY = pl.BlockSpec(memory_space=pl.ANY)
VMEM = pl.BlockSpec(memory_space=pltpu.VMEM)


def dot(left, right):
    return jnp.dot(left, right, preferred_element_type=F32)


def contract_rows(left, right):
    return lax.dot_general(
        left, right, (((0,), (0,)), ((), ())), preferred_element_type=F32
    )


def contract_cols(left, right):
    return lax.dot_general(
        left, right, (((1,), (1,)), ((), ())), preferred_element_type=F32
    )


def gelu_both(value):
    line = 0.7978845608028654 * value
    bent = line * (1.0 + 0.044715 * (value * value))
    tanh = jnp.tanh(bent)
    half = 0.5 + 0.5 * tanh
    return value * half, half + (1.0 - tanh * tanh) * (1.5 * bent - line)


def params(mebibytes):
    return pltpu.CompilerParams(vmem_limit_bytes=mebibytes * 1024 * 1024)


def cost(flops, size):
    return pl.CostEstimate(flops=flops, bytes_accessed=size, transcendentals=0)


def taps_in(odd_ref, weights_ref, held, sems):
    odd = odd_ref[0]
    return [
        pltpu.make_async_copy(weights_ref.at[tap], held.at[i], sems.at[i])
        for i, tap in enumerate((2 * odd, 1, 2 - 2 * odd))
    ]


def forward_kernel(
    odd_ref, p0, p3, p1, p2, gain_ref, weights_ref,
    act_out, slope_out, inv_out, m0, m1, m2, m3, slope_ref,
    packed, ring, held, slope_in, inv_in, sems, in_sems, out_sems,
):
    ins = [
        pltpu.make_async_copy(source, packed.at[k], in_sems.at[k])
        for k, source in enumerate((p0, p1, p2, p3))
    ]
    copies = taps_in(odd_ref, weights_ref, held, sems)
    for copy in ins + copies:
        copy.start()
    step = 64
    for k in range(4):
        ins[k].wait()

        def some(i, carry, k=k):
            at = pl.ds(pl.multiple_of(i * step, step), step)
            rows = packed[k, at, :].astype(F32)
            inv = lax.rsqrt(jnp.mean(rows * rows, axis=-1, keepdims=True) + 1e-06)
            act, slope = gelu_both(rows * inv * gain_ref[...])
            here = pl.ds(pl.multiple_of(k * Q + i * step, step), step)
            slope_in[here, :] = slope
            inv_in[here, :] = jnp.broadcast_to(inv, (step, 128))
            ring[pl.ds(pl.multiple_of((k + 1) * Q + i * step, step), step), :] = act.astype(BF16)
            return carry

        lax.fori_loop(0, Q // step, some, 0)
    outs = [
        pltpu.make_async_copy(ring.at[pl.ds(Q, N)], act_out, out_sems.at[0]),
        pltpu.make_async_copy(slope_in, slope_out, out_sems.at[1]),
        pltpu.make_async_copy(inv_in, inv_out, out_sems.at[2]),
    ]
    for copy in outs:
        copy.start()
    ring[:Q] = ring[4 * Q:5 * Q]
    ring[5 * Q:] = ring[Q:2 * Q]
    for copy in copies:
        copy.wait()
    for n in range(3):
        cols = slice(n * 256, (n + 1) * 256)
        pre = dot(ring[Q:5 * Q], held[1, :, cols])
        pre = pre + dot(ring[:4 * Q], held[0, :, cols])
        pre = pre + dot(ring[2 * Q:], held[2, :, cols])
        mid, slope = gelu_both(pre)
        slope_ref[:, cols] = slope
        for k, out in enumerate((m0, m1, m2, m3)):
            at = slice(k * Q, (k + 1) * Q)
            out[:, cols] = mid[at].astype(BF16)
    for copy in outs:
        copy.wait()


def forward(odd, pieces, gain, weights):
    shape = jax.ShapeDtypeStruct
    return pl.pallas_call(
        forward_kernel,
        in_specs=[SMEM] + [ANY] * 4 + [VMEM, ANY],
        out_specs=[ANY] * 3 + [VMEM] * 5,
        out_shape=[shape((N, C), BF16), shape((N, C), F32), shape((N, 128), F32)]
        + [shape((Q, H), BF16)] * 4
        + [shape((N, H), F32)],
        scratch_shapes=[
            pltpu.VMEM((4, Q, C), BF16),
            pltpu.VMEM((6 * Q, C), BF16),
            pltpu.VMEM((3, C, H), BF16),
            pltpu.VMEM((N, C), F32),
            pltpu.VMEM((N, 128), F32),
            pltpu.SemaphoreType.DMA((3,)),
            pltpu.SemaphoreType.DMA((4,)),
            pltpu.SemaphoreType.DMA((3,)),
        ],
        compiler_params=params(56),
        cost_estimate=cost(6 * N * C * H, 20_000_000),
        name="forward",
    )(odd, pieces[0], pieces[3], pieces[1], pieces[2], gain, weights)


def pre_grad_kernel(me_ref, core_ref, grad_ref, slope_ref, all_ref, kept_ref, away_ref):
    me, core = me_ref[0], core_ref[0]
    for k in range(4):
        at = slice(k * Q, (k + 1) * Q)
        grad = grad_ref[lax.bitwise_xor(me, k)].astype(F32)
        value = (grad * slope_ref[at, :]).astype(BF16)
        all_ref[at, :] = value
        low, high = value[:, :HALF], value[:, HALF:]
        kept_ref[at, :] = jnp.where(core == 0, low, high)
        away_ref[at, :] = jnp.where(core == 0, high, low)


def pre_grads(me, core, grads, slope):
    shape = jax.ShapeDtypeStruct
    return pl.pallas_call(
        pre_grad_kernel,
        in_specs=[SMEM] * 2 + [VMEM] * 2,
        out_specs=[VMEM] * 3,
        out_shape=[shape((N, H), BF16), shape((N, HALF), BF16), shape((N, HALF), BF16)],
        compiler_params=params(56),
        cost_estimate=cost(30_000_000_000, 5_000_000),
        name="pre_grads",
    )(me, core, grads, slope)


def backward_kernel(
    odd_ref, grad_ref, p0, p1, p2, p3, gain_ref, slope_hbm, inv_hbm, weights_ref,
    b0, b1, b2, b3, share_ref,
    ring, held, total, slope_ref, inv_ref, rows_in, sems, in_sems,
):
    copies = taps_in(odd_ref, weights_ref, held, sems)
    copies = [copies[1], copies[0], copies[2]]
    for copy in copies:
        copy.start()
    ins = [
        pltpu.make_async_copy(slope_hbm, slope_ref, in_sems.at[0]),
        pltpu.make_async_copy(inv_hbm, inv_ref, in_sems.at[1]),
    ] + [
        pltpu.make_async_copy(source, rows_in.at[k], in_sems.at[2 + k])
        for k, source in enumerate((p0, p1, p2, p3))
    ]
    for copy in ins:
        copy.start()
    ring[Q:5 * Q] = grad_ref[...]
    ring[:Q] = grad_ref[3 * Q:]
    ring[5 * Q:] = grad_ref[:Q]
    for i, copy in enumerate(copies):
        copy.wait()
        tap = (1, 0, 2)[i]
        first = (1, 2, 0)[i] * Q
        for n in range(6):
            cols = slice(n * 256, (n + 1) * 256)
            value = contract_cols(ring[first:first + N], held[tap, cols])
            total[:, cols] = value if i == 0 else total[:, cols] + value
    for copy in ins:
        copy.wait()
    step = 64
    share = jnp.zeros((8, C), F32)
    for k, out in enumerate((b0, b1, b2, b3)):

        def some(i, share, k=k, out=out):
            at = pl.ds(pl.multiple_of(i * step, step), step)
            here = pl.ds(pl.multiple_of(k * Q + i * step, step), step)
            inv = inv_ref[here, :1]
            hat = rows_in[k, at, :].astype(F32) * inv
            norm_grad = total[here, :] * slope_ref[here, :]
            product = norm_grad * hat
            mean = jnp.mean(product * gain_ref[...], axis=-1, keepdims=True)
            out[at, :] = ((norm_grad * gain_ref[...] - hat * mean) * inv).astype(BF16)
            return share + product.reshape(step // 8, 8, C).sum(0)

        share = lax.fori_loop(0, Q // step, some, share)
    share_ref[...] = jnp.sum(share, axis=0, keepdims=True)


def backward(odd, grads, pieces, gain, slope, inv, weights):
    shape = jax.ShapeDtypeStruct
    return pl.pallas_call(
        backward_kernel,
        in_specs=[SMEM, VMEM] + [ANY] * 4 + [VMEM] + [ANY] * 3,
        out_specs=[VMEM] * 5,
        out_shape=[shape((Q, C), BF16)] * 4 + [shape((1, C), F32)],
        scratch_shapes=[
            pltpu.VMEM((6 * Q, H), BF16),
            pltpu.VMEM((3, C, H), BF16),
            pltpu.VMEM((N, C), F32),
            pltpu.VMEM((N, C), F32),
            pltpu.VMEM((N, 128), F32),
            pltpu.VMEM((4, Q, C), BF16),
            pltpu.SemaphoreType.DMA((3,)),
            pltpu.SemaphoreType.DMA((6,)),
        ],
        compiler_params=params(56),
        cost_estimate=cost(1_000_000, 100_000),
        name="backward",
    )(odd, grads, *pieces, gain, slope, inv, weights)


def load_columns(own_hbm, other_hbm, both, sems):
    ins = []
    for i in range(4):
        cols = pl.ds(i * HALF, HALF)
        ins.append((
            pltpu.make_async_copy(own_hbm.at[:, cols], both.at[i, pl.ds(0, N)], sems.at[2 * i]),
            pltpu.make_async_copy(other_hbm.at[:, cols], both.at[i, pl.ds(N, N)], sems.at[2 * i + 1]),
        ))
        for copy in ins[-1]:
            copy.start()
    return ins


def kernel_share_kernel(
    odd_ref, own_hbm, other_hbm, kept_ref, came_ref, out_ref,
    both, right, rings, value, ring_sems, in_sems, out_sems,
):
    rows_in = [
        pltpu.make_async_copy(source, rings.at[i, pl.ds(Q, N)], ring_sems.at[i])
        for i, source in enumerate((kept_ref, came_ref))
    ]
    for copy in rows_in:
        copy.start()
    ins = load_columns(own_hbm, other_hbm, both, in_sems)
    odd = odd_ref[0]
    near = pl.multiple_of(jnp.where(odd == 0, 2 * Q, 0), Q)
    far = pl.multiple_of(jnp.where(odd == 0, 0, 2 * Q), Q)
    for i in range(2):
        rows_in[i].wait()
        rings[i, :Q] = rings[i, 4 * Q:5 * Q]
        rings[i, 5 * Q:] = rings[i, Q:2 * Q]
        rows = slice(i * N, (i + 1) * N)
        right[rows, :HALF] = rings[i, pl.ds(near, N), :]
        right[rows, HALF:2 * HALF] = rings[i, Q:5 * Q]
        right[rows, 2 * HALF:] = rings[i, pl.ds(far, N), :]
    outs = []
    for i in range(4):
        for copy in ins[i]:
            copy.wait()
        part = contract_rows(both[i], right[...]).astype(BF16)
        for b in range(9):
            value[2 * i:2 * i + 2, :, 48 * b:48 * b + 48, :] = part[
                :, 128 * b:128 * b + 128
            ].reshape(2, 4, 48, 128)
        for g in (2 * i, 2 * i + 1):
            outs.append(
                pltpu.make_async_copy(value.at[g], out_ref.at[:, g], out_sems.at[g])
            )
            outs[-1].start()
    for copy in outs:
        copy.wait()


def kernel_shares(odd, own, other, kept, came):
    return pl.pallas_call(
        kernel_share_kernel,
        in_specs=[SMEM] + [ANY] * 4,
        out_specs=ANY,
        out_shape=jax.ShapeDtypeStruct((4, 8, 432, 128), BF16),
        scratch_shapes=[
            pltpu.VMEM((4, 2 * N, HALF), BF16),
            pltpu.VMEM((2 * N, 3 * HALF), BF16),
            pltpu.VMEM((2, 6 * Q, HALF), BF16),
            pltpu.VMEM((8, 4, 432, 128), BF16),
            pltpu.SemaphoreType.DMA((2,)),
            pltpu.SemaphoreType.DMA((8,)),
            pltpu.SemaphoreType.DMA((8,)),
        ],
        compiler_params=params(56),
        cost_estimate=cost(6 * N * C * H, 10_000_000),
        name="kernel_shares",
    )(odd, own, other, kept, came)


def point_share_kernel(
    z_ref, me_ref, own_hbm, other_hbm, kept_ref, came_ref, gain_ref, d0, d1, d2, d3,
    both, right, value, in_sems, out_sems,
):
    ins = []
    for i in range(4):
        cols = pl.ds(i * HALF, HALF)
        ins.append([
            pltpu.make_async_copy(
                source.at[home_rows(me_ref, k), cols],
                both.at[i, pl.ds(side * N + k * Q, Q)],
                in_sems.at[8 * i + 4 * side + k],
            )
            for side, source in enumerate((own_hbm, other_hbm))
            for k in range(4)
        ])
        for copy in ins[-1]:
            copy.start()
    value[:, :, 144:] = gain_ref[...]
    right[:N] = kept_ref[...]
    right[N:] = came_ref[...]
    outs = []
    for i in range(4):
        for copy in ins[i]:
            copy.wait()
        part = contract_rows(both[i], right[...]).astype(BF16)
        for b in range(3):
            value[2 * i:2 * i + 2, :, 48 * b:48 * b + 48, :] = part[
                :, 128 * b:128 * b + 128
            ].reshape(2, 4, 48, 128)
        for g in (2 * i, 2 * i + 1):
            for d, out in enumerate((d0, d1, d2, d3)):
                source = value.at[g, lax.rem(z_ref[0] + d, 4)]
                outs.append(pltpu.make_async_copy(source, out.at[g], out_sems.at[len(outs)]))
                outs[-1].start()
    for copy in outs:
        copy.wait()


def point_shares(z, me, own, other, kept, came, gain):
    return pl.pallas_call(
        point_share_kernel,
        in_specs=[SMEM, SMEM, ANY, ANY, VMEM, VMEM, VMEM],
        out_specs=[ANY] * 4,
        out_shape=[jax.ShapeDtypeStruct((8, 160, 128), BF16)] * 4,
        scratch_shapes=[
            pltpu.VMEM((4, 2 * N, HALF), BF16),
            pltpu.VMEM((2 * N, HALF), BF16),
            pltpu.VMEM((8, 4, 160, 128), BF16),
            pltpu.SemaphoreType.DMA((32,)),
            pltpu.SemaphoreType.DMA((32,)),
        ],
        compiler_params=params(56),
        cost_estimate=cost(2 * N * C * H, 6_000_000),
        name="point_shares",
    )(z, me, own, other, kept, came, gain)


def four_sum(a, b, c, d):
    return ((a.astype(F32) + b.astype(F32)) + (c.astype(F32) + d.astype(F32))).astype(BF16)


def tap_sum_kernel(shares_ref, out_ref):
    out_ref[...] = four_sum(*[shares_ref[i] for i in range(4)])


def tap_sums(shares):
    return pl.pallas_call(
        tap_sum_kernel,
        grid=(4,),
        in_specs=[pl.BlockSpec((4, 2, 432, 128), lambda g: (0, g, 0, 0))],
        out_specs=pl.BlockSpec((2, 432, 128), lambda g: (g, 0, 0)),
        out_shape=jax.ShapeDtypeStruct((8, 432, 128), BF16),
        compiler_params=params(32),
        cost_estimate=cost(3_000_000, 5_000_000),
        name="tap_sums",
    )(shares)


def plane_kernel(taps_ref, d0, d1, d2, d3, out_ref):
    point = four_sum(d0[...], d1[...], d2[...], d3[...])
    out_ref[:, 0, :288] = taps_ref[:, :288]
    out_ref[:, 1, :144] = taps_ref[:, 288:]
    out_ref[:, 1, 144:288] = point[:, :144]
    for chip in range(2):
        out_ref[:, chip, 288:] = point[:, 144:]


def plane_shares(taps, points):
    return pl.pallas_call(
        plane_kernel,
        in_specs=[VMEM] * 5,
        out_specs=VMEM,
        out_shape=jax.ShapeDtypeStruct((8, 2, 304, 128), BF16),
        compiler_params=params(32),
        cost_estimate=cost(1_000_000, 3_000_000),
        name="plane_shares",
    )(taps, *points)


def home_rows(me_ref, k):
    return pl.ds(pl.multiple_of(lax.bitwise_xor(me_ref[0], k) * Q, Q), Q)


def stream_out_kernel(
    me_ref, m0, m1, m2, m3, point_ref, stream_ref, out_ref,
    mid, point, rows, result, in_sems, out_sems,
):
    ins = [pltpu.make_async_copy(point_ref, point, in_sems.at[8])]
    for k, source in enumerate((m0, m1, m2, m3)):
        at = pl.ds(k * Q, Q)
        ins.append(pltpu.make_async_copy(source, mid.at[at], in_sems.at[k]))
        ins.append(
            pltpu.make_async_copy(stream_ref.at[home_rows(me_ref, k)], rows.at[at], in_sems.at[4 + k])
        )
    for copy in ins:
        copy.start()
    for copy in ins:
        copy.wait()
    for n in range(6):
        cols = slice(n * 256, (n + 1) * 256)
        result[:, cols] = (rows[:, cols].astype(F32) + dot(mid[...], point[:, cols])).astype(BF16)
    outs = [
        pltpu.make_async_copy(
            result.at[pl.ds(k * Q, Q)], out_ref.at[home_rows(me_ref, k)], out_sems.at[k]
        )
        for k in range(4)
    ]
    for copy in outs:
        copy.start()
    for copy in outs:
        copy.wait()


def home_stream_out(me, mid, point_kernel, stream):
    return pl.pallas_call(
        stream_out_kernel,
        in_specs=[SMEM] + [ANY] * 6,
        out_specs=ANY,
        out_shape=jax.ShapeDtypeStruct((N, C), BF16),
        scratch_shapes=[
            pltpu.VMEM((N, H), BF16),
            pltpu.VMEM((H, C), BF16),
            pltpu.VMEM((N, C), BF16),
            pltpu.VMEM((N, C), BF16),
            pltpu.SemaphoreType.DMA((9,)),
            pltpu.SemaphoreType.DMA((4,)),
        ],
        compiler_params=params(56),
        cost_estimate=cost(2 * N * C * H, 6_000_000),
        name="stream_out",
    )(me, *mid, point_kernel, stream)


def stream_grad_kernel(
    me_ref, b0, b1, b2, b3, cotan_ref, out_ref, back, rows, in_sems, out_sems
):
    ins = []
    for k, source in enumerate((b0, b1, b2, b3)):
        ins.append((
            pltpu.make_async_copy(source, back.at[k], in_sems.at[k]),
            pltpu.make_async_copy(cotan_ref.at[home_rows(me_ref, k)], rows.at[k], in_sems.at[4 + k]),
        ))
        for copy in ins[-1]:
            copy.start()
    outs = []
    for k in range(4):
        for copy in ins[k]:
            copy.wait()
        rows[k] = (rows[k].astype(F32) + back[k].astype(F32)).astype(BF16)
        outs.append(
            pltpu.make_async_copy(rows.at[k], out_ref.at[home_rows(me_ref, k)], out_sems.at[k])
        )
        outs[-1].start()
    for copy in outs:
        copy.wait()


def home_stream_grad(me, back, cotan):
    return pl.pallas_call(
        stream_grad_kernel,
        in_specs=[SMEM] + [ANY] * 5,
        out_specs=ANY,
        out_shape=jax.ShapeDtypeStruct((N, C), BF16),
        scratch_shapes=[
            pltpu.VMEM((4, Q, C), BF16),
            pltpu.VMEM((4, Q, C), BF16),
            pltpu.SemaphoreType.DMA((8,)),
            pltpu.SemaphoreType.DMA((4,)),
        ],
        compiler_params=params(56),
        cost_estimate=cost(2 * N * C, 5_000_000),
        name="stream_grad",
    )(me, *back, cotan)


def swap_core(value):
    return lax.ppermute(value, "core", [(0, 1), (1, 0)])


def partner(value, k):
    return lax.ppermute(value, GROUP, [(i, i ^ k) for i in range(4)])


def exchange(pieces):
    return [pieces[0]] + [partner(pieces[k], k) for k in range(1, len(pieces))]


def shards(stream, norm_gain_vector, conv_kernel, point_kernel, out_grad):
    core = lax.axis_index("core").astype(jnp.int32)
    odd = lax.axis_index("yh").astype(jnp.int32)
    me = 2 * lax.axis_index("xh") + odd
    z = lax.axis_index("z").astype(jnp.int32)
    core_word, odd_word, z_word = core.reshape(1), odd.reshape(1), z.reshape(1)
    gain_row = norm_gain_vector.reshape(1, C)
    cotan = out_grad[0]

    me_word = me.reshape(1)
    quarters = stream[0].reshape(4, Q, C)
    pieces = exchange([lax.dynamic_index_in_dim(quarters, me ^ k, 0, False) for k in range(4)])
    mid_grad = contract_cols(cotan, point_kernel).astype(BF16).reshape(4, Q, H)
    _, *pieces = lax.optimization_barrier((mid_grad, *pieces))
    mid_grad = lax.all_to_all(mid_grad, GROUP, 0, 0, tiled=True)
    cotan_other = swap_core(cotan)

    act, slope_in, inv, m0, m1, m2, m3, slope = forward(
        odd_word, pieces, gain_row, conv_kernel
    )
    mid_grad, slope = lax.optimization_barrier((mid_grad, slope))
    pre_grad, kept, away = pre_grads(me_word, core_word, mid_grad, slope)
    act_other = swap_core(act)
    came = swap_core(away)
    shares = kernel_shares(odd_word, act, act_other, kept, came)
    shares, pre_grad, m0, m1, m2, m3 = lax.optimization_barrier(
        (shares, pre_grad, m0, m1, m2, m3)
    )
    shares = lax.all_to_all(shares, "z", 0, 0, tiled=True)
    mid = exchange([m0, m1, m2, m3])
    b0, b1, b2, b3, gain = backward(
        odd_word, pre_grad, pieces, gain_row, slope_in, inv, conv_kernel
    )
    back = exchange([b0, b1, b2, b3])
    gain, *mid = lax.optimization_barrier((gain, *mid))
    mid_home = jnp.concatenate(mid)
    low, high = mid_home[:, :HALF], mid_home[:, HALF:]
    mid_kept = jnp.where(core == 0, low, high)
    mid_came = swap_core(jnp.where(core == 0, high, low))
    gain = gain.astype(BF16).reshape(8, 4, 1, 48)
    gain = jnp.pad(gain, ((0, 0), (0, 0), (0, 15), (0, 80)))
    points = list(
        point_shares(z_word, me_word, cotan, cotan_other, mid_kept, mid_came, gain)
    )
    points[0], points[1], points[2], points[3], back[1], back[2], *mid = lax.optimization_barrier(
        (*points, back[1], back[2], *mid)
    )
    points = [points[0]] + [
        lax.ppermute(points[d], "z", [(i, (i + d) % 4) for i in range(4)]) for d in (1, 2, 3)
    ]
    stream_out = home_stream_out(me_word, mid, point_kernel, stream[0])
    shares, stream_out = lax.optimization_barrier((shares, stream_out))
    taps = tap_sums(shares)
    stream_grad = home_stream_grad(me_word, back, cotan)
    taps, stream_grad, *points = lax.optimization_barrier((taps, stream_grad, *points))
    plane = plane_shares(taps, points).reshape(16, 304, 128)
    plane = lax.all_to_all(plane, PLANE, 0, 0, tiled=True)
    plane = jnp.sum(plane.astype(F32), axis=0)[:296]
    whole = lax.all_gather(plane, ("xl", "core"))
    gain_grad = whole[0, 288, :48] + whole[1, 288, :48]
    whole = whole[:, :288].reshape(2, 2, 2, 3, 48, 128).transpose(0, 2, 4, 1, 3, 5)
    whole = whole.reshape(4, 48, H)
    kernel_grad = jnp.stack([whole[0], whole[1], whole[2]])
    return (stream_out[None], stream_grad[None], kernel_grad, whole[3].T, gain_grad)


def solution(mesh):
    fine = Mesh(
        mesh.devices.reshape(2, 2, 2, 4, 2, 2), ("xh", "yh", "yl", "z", "xl", "core")
    )
    ctx, rep = ("xh", "yh", "yl", "z"), ("xl", "core")
    placed = (P(rep, ctx, None), P(), P(), P(), P(rep, ctx, None))
    return jax.shard_map(
        shards,
        mesh=fine,
        in_specs=placed,
        out_specs=(
            P(rep, ctx, None),
            P(rep, ctx, None),
            P(None, ctx, None),
            P(None, ctx),
            P(ctx),
        ),
        check_vma=False,
    )
```

```python
import functools

import jax
import jax.numpy as jnp
from jax import lax
from jax.experimental import pallas as pl
from jax.experimental.pallas import tpu as pltpu
from jax.sharding import Mesh, PartitionSpec as P

F32 = jnp.float32
BF16 = jnp.bfloat16
PLANE = ("xh", "yh", "yl", "xl")
GROUP = ("xh", "yh")
Q = 128
N = 512
C = 1536
H = 768
HALF = 384
SMEM = pl.BlockSpec(memory_space=pltpu.SMEM)
ANY = pl.BlockSpec(memory_space=pl.ANY)
VMEM = pl.BlockSpec(memory_space=pltpu.VMEM)


def dot(left, right):
    return jnp.dot(left, right, preferred_element_type=F32)


def contract_rows(left, right):
    return lax.dot_general(
        left, right, (((0,), (0,)), ((), ())), preferred_element_type=F32
    )


def contract_cols(left, right):
    return lax.dot_general(
        left, right, (((1,), (1,)), ((), ())), preferred_element_type=F32
    )


def gelu_both(value):
    line = 0.7978845608028654 * value
    bent = line * (1.0 + 0.044715 * (value * value))
    tanh = jnp.tanh(bent)
    half = 0.5 + 0.5 * tanh
    return value * half, half + (1.0 - tanh * tanh) * (1.5 * bent - line)


def params(mebibytes):
    return pltpu.CompilerParams(vmem_limit_bytes=mebibytes * 1024 * 1024)


def cost(flops, size):
    return pl.CostEstimate(flops=flops, bytes_accessed=size, transcendentals=0)


def taps_in(odd_ref, weights_ref, held, sems):
    odd = odd_ref[0]
    return [
        pltpu.make_async_copy(weights_ref.at[tap], held.at[i], sems.at[i])
        for i, tap in enumerate((2 * odd, 1, 2 - 2 * odd))
    ]


def forward_kernel(
    odd_ref, p0, p3, p1, p2, gain_ref, weights_ref,
    act_out, slope_out, inv_out, m0, m1, m2, m3, slope_ref,
    packed, ring, held, slope_in, inv_in, sems, in_sems, out_sems,
):
    ins = [
        pltpu.make_async_copy(source, packed.at[k], in_sems.at[k])
        for k, source in enumerate((p0, p1, p2, p3))
    ]
    copies = taps_in(odd_ref, weights_ref, held, sems)
    for copy in ins + copies:
        copy.start()
    step = 64
    for k in range(4):
        ins[k].wait()

        def some(i, carry, k=k):
            at = pl.ds(pl.multiple_of(i * step, step), step)
            rows = packed[k, at, :].astype(F32)
            inv = lax.rsqrt(jnp.mean(rows * rows, axis=-1, keepdims=True) + 1e-06)
            act, slope = gelu_both(rows * inv * gain_ref[...])
            here = pl.ds(pl.multiple_of(k * Q + i * step, step), step)
            slope_in[here, :] = slope
            inv_in[here, :] = jnp.broadcast_to(inv, (step, 128))
            ring[pl.ds(pl.multiple_of((k + 1) * Q + i * step, step), step), :] = act.astype(BF16)
            return carry

        lax.fori_loop(0, Q // step, some, 0)
    outs = [
        pltpu.make_async_copy(ring.at[pl.ds(Q, N)], act_out, out_sems.at[0]),
        pltpu.make_async_copy(slope_in, slope_out, out_sems.at[1]),
        pltpu.make_async_copy(inv_in, inv_out, out_sems.at[2]),
    ]
    for copy in outs:
        copy.start()
    ring[:Q] = ring[4 * Q:5 * Q]
    ring[5 * Q:] = ring[Q:2 * Q]
    for copy in copies:
        copy.wait()
    for n in range(3):
        cols = slice(n * 256, (n + 1) * 256)
        pre = dot(ring[Q:5 * Q], held[1, :, cols])
        pre = pre + dot(ring[:4 * Q], held[0, :, cols])
        pre = pre + dot(ring[2 * Q:], held[2, :, cols])
        mid, slope = gelu_both(pre)
        slope_ref[:, cols] = slope
        for k, out in enumerate((m0, m1, m2, m3)):
            at = slice(k * Q, (k + 1) * Q)
            out[:, cols] = mid[at].astype(BF16)
    for copy in outs:
        copy.wait()


def forward(odd, pieces, gain, weights):
    shape = jax.ShapeDtypeStruct
    return pl.pallas_call(
        forward_kernel,
        in_specs=[SMEM] + [ANY] * 4 + [VMEM, ANY],
        out_specs=[ANY] * 3 + [VMEM] * 5,
        out_shape=[shape((N, C), BF16), shape((N, C), F32), shape((N, 128), F32)]
        + [shape((Q, H), BF16)] * 4
        + [shape((N, H), F32)],
        scratch_shapes=[
            pltpu.VMEM((4, Q, C), BF16),
            pltpu.VMEM((6 * Q, C), BF16),
            pltpu.VMEM((3, C, H), BF16),
            pltpu.VMEM((N, C), F32),
            pltpu.VMEM((N, 128), F32),
            pltpu.SemaphoreType.DMA((3,)),
            pltpu.SemaphoreType.DMA((4,)),
            pltpu.SemaphoreType.DMA((3,)),
        ],
        compiler_params=params(56),
        cost_estimate=cost(6 * N * C * H, 20_000_000),
        name="forward",
    )(odd, pieces[0], pieces[3], pieces[1], pieces[2], gain, weights)


def pre_grad_kernel(me_ref, core_ref, grad_ref, slope_ref, all_ref, kept_ref, away_ref):
    me, core = me_ref[0], core_ref[0]
    for k in range(4):
        at = slice(k * Q, (k + 1) * Q)
        grad = grad_ref[lax.bitwise_xor(me, k)].astype(F32)
        value = (grad * slope_ref[at, :]).astype(BF16)
        all_ref[at, :] = value
        low, high = value[:, :HALF], value[:, HALF:]
        kept_ref[at, :] = jnp.where(core == 0, low, high)
        away_ref[at, :] = jnp.where(core == 0, high, low)


def pre_grads(me, core, grads, slope):
    shape = jax.ShapeDtypeStruct
    return pl.pallas_call(
        pre_grad_kernel,
        in_specs=[SMEM] * 2 + [VMEM] * 2,
        out_specs=[VMEM] * 3,
        out_shape=[shape((N, H), BF16), shape((N, HALF), BF16), shape((N, HALF), BF16)],
        compiler_params=params(56),
        cost_estimate=cost(30_000_000_000, 5_000_000),
        name="pre_grads",
    )(me, core, grads, slope)


def backward_kernel(
    odd_ref, grad_ref, p0, p1, p2, p3, gain_ref, slope_hbm, inv_hbm, weights_ref,
    b0, b1, b2, b3, share_ref,
    ring, held, total, slope_ref, inv_ref, rows_in, sems, in_sems,
):
    copies = taps_in(odd_ref, weights_ref, held, sems)
    copies = [copies[1], copies[0], copies[2]]
    for copy in copies:
        copy.start()
    ins = [
        pltpu.make_async_copy(slope_hbm, slope_ref, in_sems.at[0]),
        pltpu.make_async_copy(inv_hbm, inv_ref, in_sems.at[1]),
    ] + [
        pltpu.make_async_copy(source, rows_in.at[k], in_sems.at[2 + k])
        for k, source in enumerate((p0, p1, p2, p3))
    ]
    for copy in ins:
        copy.start()
    ring[Q:5 * Q] = grad_ref[...]
    ring[:Q] = grad_ref[3 * Q:]
    ring[5 * Q:] = grad_ref[:Q]
    for i, copy in enumerate(copies):
        copy.wait()
        tap = (1, 0, 2)[i]
        first = (1, 2, 0)[i] * Q
        for n in range(6):
            cols = slice(n * 256, (n + 1) * 256)
            value = contract_cols(ring[first:first + N], held[tap, cols])
            total[:, cols] = value if i == 0 else total[:, cols] + value
    for copy in ins:
        copy.wait()
    step = 64
    share = jnp.zeros((8, C), F32)
    for k, out in enumerate((b0, b1, b2, b3)):

        def some(i, share, k=k, out=out):
            at = pl.ds(pl.multiple_of(i * step, step), step)
            here = pl.ds(pl.multiple_of(k * Q + i * step, step), step)
            inv = inv_ref[here, :1]
            hat = rows_in[k, at, :].astype(F32) * inv
            norm_grad = total[here, :] * slope_ref[here, :]
            product = norm_grad * hat
            mean = jnp.mean(product * gain_ref[...], axis=-1, keepdims=True)
            out[at, :] = ((norm_grad * gain_ref[...] - hat * mean) * inv).astype(BF16)
            return share + product.reshape(step // 8, 8, C).sum(0)

        share = lax.fori_loop(0, Q // step, some, share)
    share_ref[...] = jnp.sum(share, axis=0, keepdims=True)


def backward(odd, grads, pieces, gain, slope, inv, weights):
    shape = jax.ShapeDtypeStruct
    return pl.pallas_call(
        backward_kernel,
        in_specs=[SMEM, VMEM] + [ANY] * 4 + [VMEM] + [ANY] * 3,
        out_specs=[VMEM] * 5,
        out_shape=[shape((Q, C), BF16)] * 4 + [shape((1, C), F32)],
        scratch_shapes=[
            pltpu.VMEM((6 * Q, H), BF16),
            pltpu.VMEM((3, C, H), BF16),
            pltpu.VMEM((N, C), F32),
            pltpu.VMEM((N, C), F32),
            pltpu.VMEM((N, 128), F32),
            pltpu.VMEM((4, Q, C), BF16),
            pltpu.SemaphoreType.DMA((3,)),
            pltpu.SemaphoreType.DMA((6,)),
        ],
        compiler_params=params(56),
        cost_estimate=cost(1_000_000, 100_000),
        name="backward",
    )(odd, grads, *pieces, gain, slope, inv, weights)


def load_columns(own_hbm, other_hbm, both, sems):
    ins = []
    for i in range(4):
        cols = pl.ds(i * HALF, HALF)
        ins.append((
            pltpu.make_async_copy(own_hbm.at[:, cols], both.at[i, pl.ds(0, N)], sems.at[2 * i]),
            pltpu.make_async_copy(other_hbm.at[:, cols], both.at[i, pl.ds(N, N)], sems.at[2 * i + 1]),
        ))
        for copy in ins[-1]:
            copy.start()
    return ins


def kernel_share_kernel(
    odd_ref, own_hbm, other_hbm, kept_ref, came_ref, out_ref,
    both, right, rings, value, ring_sems, in_sems, out_sems,
):
    rows_in = [
        pltpu.make_async_copy(source, rings.at[i, pl.ds(Q, N)], ring_sems.at[i])
        for i, source in enumerate((kept_ref, came_ref))
    ]
    for copy in rows_in:
        copy.start()
    ins = load_columns(own_hbm, other_hbm, both, in_sems)
    odd = odd_ref[0]
    near = pl.multiple_of(jnp.where(odd == 0, 2 * Q, 0), Q)
    far = pl.multiple_of(jnp.where(odd == 0, 0, 2 * Q), Q)
    for i in range(2):
        rows_in[i].wait()
        rings[i, :Q] = rings[i, 4 * Q:5 * Q]
        rings[i, 5 * Q:] = rings[i, Q:2 * Q]
        rows = slice(i * N, (i + 1) * N)
        right[rows, :HALF] = rings[i, pl.ds(near, N), :]
        right[rows, HALF:2 * HALF] = rings[i, Q:5 * Q]
        right[rows, 2 * HALF:] = rings[i, pl.ds(far, N), :]
    outs = []
    for i in range(4):
        for copy in ins[i]:
            copy.wait()
        part = contract_rows(both[i], right[...]).astype(BF16)
        for b in range(9):
            value[2 * i:2 * i + 2, :, 48 * b:48 * b + 48, :] = part[
                :, 128 * b:128 * b + 128
            ].reshape(2, 4, 48, 128)
        for g in (2 * i, 2 * i + 1):
            outs.append(
                pltpu.make_async_copy(value.at[g], out_ref.at[:, g], out_sems.at[g])
            )
            outs[-1].start()
    for copy in outs:
        copy.wait()


def kernel_shares(odd, own, other, kept, came):
    return pl.pallas_call(
        kernel_share_kernel,
        in_specs=[SMEM] + [ANY] * 4,
        out_specs=ANY,
        out_shape=jax.ShapeDtypeStruct((4, 8, 432, 128), BF16),
        scratch_shapes=[
            pltpu.VMEM((4, 2 * N, HALF), BF16),
            pltpu.VMEM((2 * N, 3 * HALF), BF16),
            pltpu.VMEM((2, 6 * Q, HALF), BF16),
            pltpu.VMEM((8, 4, 432, 128), BF16),
            pltpu.SemaphoreType.DMA((2,)),
            pltpu.SemaphoreType.DMA((8,)),
            pltpu.SemaphoreType.DMA((8,)),
        ],
        compiler_params=params(56),
        cost_estimate=cost(6 * N * C * H, 10_000_000),
        name="kernel_shares",
    )(odd, own, other, kept, came)


def point_share_kernel(
    z_ref, me_ref, own_hbm, other_hbm, kept_ref, came_ref, gain_ref, d0, d1, d2, d3,
    both, right, value, in_sems, out_sems,
):
    ins = []
    for i in range(4):
        cols = pl.ds(i * HALF, HALF)
        ins.append([
            pltpu.make_async_copy(
                source.at[home_rows(me_ref, k), cols],
                both.at[i, pl.ds(side * N + k * Q, Q)],
                in_sems.at[8 * i + 4 * side + k],
            )
            for side, source in enumerate((own_hbm, other_hbm))
            for k in range(4)
        ])
        for copy in ins[-1]:
            copy.start()
    value[:, :, 144:] = gain_ref[...]
    right[:N] = kept_ref[...]
    right[N:] = came_ref[...]
    outs = []
    for i in range(4):
        for copy in ins[i]:
            copy.wait()
        part = contract_rows(both[i], right[...]).astype(BF16)
        for b in range(3):
            value[2 * i:2 * i + 2, :, 48 * b:48 * b + 48, :] = part[
                :, 128 * b:128 * b + 128
            ].reshape(2, 4, 48, 128)
        for g in (2 * i, 2 * i + 1):
            for d, out in enumerate((d0, d1, d2, d3)):
                source = value.at[g, lax.rem(z_ref[0] + d, 4)]
                outs.append(pltpu.make_async_copy(source, out.at[g], out_sems.at[len(outs)]))
                outs[-1].start()
    for copy in outs:
        copy.wait()


def point_shares(z, me, own, other, kept, came, gain):
    return pl.pallas_call(
        point_share_kernel,
        in_specs=[SMEM, SMEM, ANY, ANY, VMEM, VMEM, VMEM],
        out_specs=[ANY] * 4,
        out_shape=[jax.ShapeDtypeStruct((8, 160, 128), BF16)] * 4,
        scratch_shapes=[
            pltpu.VMEM((4, 2 * N, HALF), BF16),
            pltpu.VMEM((2 * N, HALF), BF16),
            pltpu.VMEM((8, 4, 160, 128), BF16),
            pltpu.SemaphoreType.DMA((32,)),
            pltpu.SemaphoreType.DMA((32,)),
        ],
        compiler_params=params(56),
        cost_estimate=cost(2 * N * C * H, 6_000_000),
        name="point_shares",
    )(z, me, own, other, kept, came, gain)


def four_sum(a, b, c, d):
    return ((a.astype(F32) + b.astype(F32)) + (c.astype(F32) + d.astype(F32))).astype(BF16)


def tap_sum_kernel(shares_ref, out_ref):
    out_ref[...] = four_sum(*[shares_ref[i] for i in range(4)])


def tap_sums(shares):
    return pl.pallas_call(
        tap_sum_kernel,
        grid=(4,),
        in_specs=[pl.BlockSpec((4, 2, 432, 128), lambda g: (0, g, 0, 0))],
        out_specs=pl.BlockSpec((2, 432, 128), lambda g: (g, 0, 0)),
        out_shape=jax.ShapeDtypeStruct((8, 432, 128), BF16),
        compiler_params=params(32),
        cost_estimate=cost(3_000_000, 5_000_000),
        name="tap_sums",
    )(shares)


def plane_kernel(taps_ref, d0, d1, d2, d3, out_ref):
    point = four_sum(d0[...], d1[...], d2[...], d3[...])
    out_ref[:, 0, :288] = taps_ref[:, :288]
    out_ref[:, 1, :144] = taps_ref[:, 288:]
    out_ref[:, 1, 144:288] = point[:, :144]
    for chip in range(2):
        out_ref[:, chip, 288:] = point[:, 144:]


def plane_shares(taps, points):
    return pl.pallas_call(
        plane_kernel,
        in_specs=[VMEM] * 5,
        out_specs=VMEM,
        out_shape=jax.ShapeDtypeStruct((8, 2, 304, 128), BF16),
        compiler_params=params(32),
        cost_estimate=cost(1_000_000, 3_000_000),
        name="plane_shares",
    )(taps, *points)


def mid_half_kernel(core_ref, m0, m1, m2, m3, kept_ref, away_ref):
    core = core_ref[0]
    for k, source in enumerate((m0, m1, m2, m3)):
        at = slice(k * Q, (k + 1) * Q)
        low, high = source[:, :HALF], source[:, HALF:]
        kept_ref[at, :] = jnp.where(core == 0, low, high)
        away_ref[at, :] = jnp.where(core == 0, high, low)


def mid_halves(core, mid):
    shape = jax.ShapeDtypeStruct
    return pl.pallas_call(
        mid_half_kernel,
        in_specs=[SMEM] + [VMEM] * 4,
        out_specs=[VMEM] * 2,
        out_shape=[shape((N, HALF), BF16)] * 2,
        compiler_params=params(56),
        cost_estimate=cost(N * H, 2_000_000),
        name="mid_halves",
    )(core, *mid)


def unpack_kernel(whole_ref, kernel_ref, point_ref, gain_ref):
    for core in range(2):
        for b in range(3):
            cols = slice(core * HALF + b * 128, core * HALF + b * 128 + 128)
            first, second = slice(48 * b, 48 * b + 48), slice(144 + 48 * b, 192 + 48 * b)
            kernel_ref[0, :, cols] = whole_ref[core, first]
            kernel_ref[1, :, cols] = whole_ref[core, second]
            kernel_ref[2, :, cols] = whole_ref[2 + core, first]
            point_ref[:, cols] = whole_ref[2 + core, second]
    gain_ref[...] = whole_ref[0, 288:296] + whole_ref[1, 288:296]


def unpacked(whole):
    shape = jax.ShapeDtypeStruct
    return pl.pallas_call(
        unpack_kernel,
        in_specs=[VMEM],
        out_specs=[VMEM] * 3,
        out_shape=[shape((3, 48, H), F32), shape((48, H), F32), shape((8, 128), F32)],
        compiler_params=params(32),
        cost_estimate=cost(1_000_000, 1_200_000),
        name="unpack",
    )(whole)


def home_rows(me_ref, k):
    return pl.ds(pl.multiple_of(lax.bitwise_xor(me_ref[0], k) * Q, Q), Q)


def stream_out_kernel(
    me_ref, m0, m1, m2, m3, point_ref, stream_ref, out_ref,
    mid, point, rows, result, in_sems, out_sems,
):
    ins = [pltpu.make_async_copy(point_ref, point, in_sems.at[8])]
    for k, source in enumerate((m0, m1, m2, m3)):
        at = pl.ds(k * Q, Q)
        ins.append(pltpu.make_async_copy(source, mid.at[at], in_sems.at[k]))
        ins.append(
            pltpu.make_async_copy(stream_ref.at[home_rows(me_ref, k)], rows.at[at], in_sems.at[4 + k])
        )
    for copy in ins:
        copy.start()
    for copy in ins:
        copy.wait()
    for n in range(6):
        cols = slice(n * 256, (n + 1) * 256)
        result[:, cols] = (rows[:, cols].astype(F32) + dot(mid[...], point[:, cols])).astype(BF16)
    outs = [
        pltpu.make_async_copy(
            result.at[pl.ds(k * Q, Q)], out_ref.at[home_rows(me_ref, k)], out_sems.at[k]
        )
        for k in range(4)
    ]
    for copy in outs:
        copy.start()
    for copy in outs:
        copy.wait()


def home_stream_out(me, mid, point_kernel, stream):
    return pl.pallas_call(
        stream_out_kernel,
        in_specs=[SMEM] + [ANY] * 6,
        out_specs=ANY,
        out_shape=jax.ShapeDtypeStruct((N, C), BF16),
        scratch_shapes=[
            pltpu.VMEM((N, H), BF16),
            pltpu.VMEM((H, C), BF16),
            pltpu.VMEM((N, C), BF16),
            pltpu.VMEM((N, C), BF16),
            pltpu.SemaphoreType.DMA((9,)),
            pltpu.SemaphoreType.DMA((4,)),
        ],
        compiler_params=params(56),
        cost_estimate=cost(2 * N * C * H, 6_000_000),
        name="stream_out",
    )(me, *mid, point_kernel, stream)


def stream_grad_kernel(
    me_ref, b0, b1, b2, b3, cotan_ref, out_ref, back, rows, in_sems, out_sems
):
    ins = []
    for k, source in enumerate((b0, b1, b2, b3)):
        ins.append((
            pltpu.make_async_copy(source, back.at[k], in_sems.at[k]),
            pltpu.make_async_copy(cotan_ref.at[home_rows(me_ref, k)], rows.at[k], in_sems.at[4 + k]),
        ))
        for copy in ins[-1]:
            copy.start()
    outs = []
    for k in range(4):
        for copy in ins[k]:
            copy.wait()
        rows[k] = (rows[k].astype(F32) + back[k].astype(F32)).astype(BF16)
        outs.append(
            pltpu.make_async_copy(rows.at[k], out_ref.at[home_rows(me_ref, k)], out_sems.at[k])
        )
        outs[-1].start()
    for copy in outs:
        copy.wait()


def home_stream_grad(me, back, cotan):
    return pl.pallas_call(
        stream_grad_kernel,
        in_specs=[SMEM] + [ANY] * 5,
        out_specs=ANY,
        out_shape=jax.ShapeDtypeStruct((N, C), BF16),
        scratch_shapes=[
            pltpu.VMEM((4, Q, C), BF16),
            pltpu.VMEM((4, Q, C), BF16),
            pltpu.SemaphoreType.DMA((8,)),
            pltpu.SemaphoreType.DMA((4,)),
        ],
        compiler_params=params(56),
        cost_estimate=cost(2 * N * C, 5_000_000),
        name="stream_grad",
    )(me, *back, cotan)


def swap_core(value):
    return lax.ppermute(value, "core", [(0, 1), (1, 0)])


def partner(value, k):
    return lax.ppermute(value, GROUP, [(i, i ^ k) for i in range(4)])


def exchange(pieces):
    return [pieces[0]] + [partner(pieces[k], k) for k in range(1, len(pieces))]


def shards(stream, norm_gain_vector, conv_kernel, point_kernel, out_grad):
    core = lax.axis_index("core").astype(jnp.int32)
    odd = lax.axis_index("yh").astype(jnp.int32)
    me = 2 * lax.axis_index("xh") + odd
    z = lax.axis_index("z").astype(jnp.int32)
    core_word, odd_word, z_word = core.reshape(1), odd.reshape(1), z.reshape(1)
    gain_row = norm_gain_vector.reshape(1, C)
    cotan = out_grad[0]

    me_word = me.reshape(1)
    quarters = stream[0].reshape(4, Q, C)
    pieces = exchange([lax.dynamic_index_in_dim(quarters, me ^ k, 0, False) for k in range(4)])
    mid_grad = contract_cols(cotan, point_kernel).astype(BF16).reshape(4, Q, H)
    _, *pieces = lax.optimization_barrier((mid_grad, *pieces))
    mid_grad = lax.all_to_all(mid_grad, GROUP, 0, 0, tiled=True)
    cotan_other = swap_core(cotan)

    act, slope_in, inv, m0, m1, m2, m3, slope = forward(
        odd_word, pieces, gain_row, conv_kernel
    )
    mid_grad, slope = lax.optimization_barrier((mid_grad, slope))
    pre_grad, kept, away = pre_grads(me_word, core_word, mid_grad, slope)
    act_other = swap_core(act)
    came = swap_core(away)
    shares = kernel_shares(odd_word, act, act_other, kept, came)
    shares, pre_grad, m0, m1, m2, m3 = lax.optimization_barrier(
        (shares, pre_grad, m0, m1, m2, m3)
    )
    shares = lax.all_to_all(shares, "z", 0, 0, tiled=True)
    mid = exchange([m0, m1, m2, m3])
    b0, b1, b2, b3, gain = backward(
        odd_word, pre_grad, pieces, gain_row, slope_in, inv, conv_kernel
    )
    back = exchange([b0, b1, b2, b3])
    gain, *mid = lax.optimization_barrier((gain, *mid))
    mid_kept, mid_away = mid_halves(core_word, mid)
    mid_came = swap_core(mid_away)
    gain = gain.astype(BF16).reshape(8, 4, 1, 48)
    gain = jnp.pad(gain, ((0, 0), (0, 0), (0, 15), (0, 80)))
    points = list(
        point_shares(z_word, me_word, cotan, cotan_other, mid_kept, mid_came, gain)
    )
    points[0], points[1], points[2], points[3], back[1], back[2], *mid = lax.optimization_barrier(
        (*points, back[1], back[2], *mid)
    )
    points = [points[0]] + [
        lax.ppermute(points[d], "z", [(i, (i + d) % 4) for i in range(4)]) for d in (1, 2, 3)
    ]
    stream_out = home_stream_out(me_word, mid, point_kernel, stream[0])
    shares, stream_out = lax.optimization_barrier((shares, stream_out))
    taps = tap_sums(shares)
    stream_grad = home_stream_grad(me_word, back, cotan)
    taps, stream_grad, *points = lax.optimization_barrier((taps, stream_grad, *points))
    plane = plane_shares(taps, points).reshape(16, 304, 128)
    plane = lax.all_to_all(plane, PLANE, 0, 0, tiled=True)
    plane = jnp.sum(plane.astype(F32), axis=0)[:296]
    whole = lax.all_gather(plane, ("xl", "core"))
    kernel_grad, point_grad, gain_grad = unpacked(whole)
    return (stream_out[None], stream_grad[None], kernel_grad, point_grad.T, gain_grad[0, :48])


def solution(mesh):
    fine = Mesh(
        mesh.devices.reshape(2, 2, 2, 4, 2, 2), ("xh", "yh", "yl", "z", "xl", "core")
    )
    ctx, rep = ("xh", "yh", "yl", "z"), ("xl", "core")
    placed = (P(rep, ctx, None), P(), P(), P(), P(rep, ctx, None))
    return jax.shard_map(
        shards,
        mesh=fine,
        in_specs=placed,
        out_specs=(
            P(rep, ctx, None),
            P(rep, ctx, None),
            P(None, ctx, None),
            P(None, ctx),
            P(ctx),
        ),
        check_vma=False,
    )
```

```python
import functools

import jax
import jax.numpy as jnp
from jax import lax
from jax.experimental import pallas as pl
from jax.experimental.pallas import tpu as pltpu
from jax.sharding import Mesh, PartitionSpec as P

F32 = jnp.float32
BF16 = jnp.bfloat16
PLANE = ("xh", "yh", "yl", "xl")
GROUP = ("xh", "yh")
Q = 128
N = 512
C = 1536
H = 768
HALF = 384
SMEM = pl.BlockSpec(memory_space=pltpu.SMEM)
ANY = pl.BlockSpec(memory_space=pl.ANY)
VMEM = pl.BlockSpec(memory_space=pltpu.VMEM)


def dot(left, right):
    return jnp.dot(left, right, preferred_element_type=F32)


def contract_rows(left, right):
    return lax.dot_general(
        left, right, (((0,), (0,)), ((), ())), preferred_element_type=F32
    )


def contract_cols(left, right):
    return lax.dot_general(
        left, right, (((1,), (1,)), ((), ())), preferred_element_type=F32
    )


def gelu_both(value):
    line = 0.7978845608028654 * value
    bent = line * (1.0 + 0.044715 * (value * value))
    tanh = jnp.tanh(bent)
    half = 0.5 + 0.5 * tanh
    return value * half, half + (1.0 - tanh * tanh) * (1.5 * bent - line)


def params(mebibytes):
    return pltpu.CompilerParams(vmem_limit_bytes=mebibytes * 1024 * 1024)


def cost(flops, size):
    return pl.CostEstimate(flops=flops, bytes_accessed=size, transcendentals=0)


def taps_in(odd_ref, weights_ref, held, sems):
    odd = odd_ref[0]
    return [
        pltpu.make_async_copy(weights_ref.at[tap], held.at[i], sems.at[i])
        for i, tap in enumerate((2 * odd, 1, 2 - 2 * odd))
    ]


def forward_kernel(
    odd_ref, p0, p3, p1, p2, gain_ref, weights_ref,
    act_out, slope_out, inv_out, m0, m1, m2, m3, slope_ref,
    packed, ring, held, slope_in, inv_in, sems, in_sems, out_sems,
):
    ins = [
        pltpu.make_async_copy(source, packed.at[k], in_sems.at[k])
        for k, source in enumerate((p0, p1, p2, p3))
    ]
    copies = taps_in(odd_ref, weights_ref, held, sems)
    for copy in ins + copies:
        copy.start()
    step = 64
    for k in range(4):
        ins[k].wait()

        def some(i, carry, k=k):
            at = pl.ds(pl.multiple_of(i * step, step), step)
            rows = packed[k, at, :].astype(F32)
            inv = lax.rsqrt(jnp.mean(rows * rows, axis=-1, keepdims=True) + 1e-06)
            act, slope = gelu_both(rows * inv * gain_ref[...])
            here = pl.ds(pl.multiple_of(k * Q + i * step, step), step)
            slope_in[here, :] = slope
            inv_in[here, :] = jnp.broadcast_to(inv, (step, 128))
            ring[pl.ds(pl.multiple_of((k + 1) * Q + i * step, step), step), :] = act.astype(BF16)
            return carry

        lax.fori_loop(0, Q // step, some, 0)
    outs = [
        pltpu.make_async_copy(ring.at[pl.ds(Q, N)], act_out, out_sems.at[0]),
        pltpu.make_async_copy(slope_in, slope_out, out_sems.at[1]),
        pltpu.make_async_copy(inv_in, inv_out, out_sems.at[2]),
    ]
    for copy in outs:
        copy.start()
    ring[:Q] = ring[4 * Q:5 * Q]
    ring[5 * Q:] = ring[Q:2 * Q]
    for copy in copies:
        copy.wait()
    for n in range(3):
        cols = slice(n * 256, (n + 1) * 256)
        pre = dot(ring[Q:5 * Q], held[1, :, cols])
        pre = pre + dot(ring[:4 * Q], held[0, :, cols])
        pre = pre + dot(ring[2 * Q:], held[2, :, cols])
        mid, slope = gelu_both(pre)
        slope_ref[:, cols] = slope
        for k, out in enumerate((m0, m1, m2, m3)):
            at = slice(k * Q, (k + 1) * Q)
            out[:, cols] = mid[at].astype(BF16)
    for copy in outs:
        copy.wait()


def forward(odd, pieces, gain, weights):
    shape = jax.ShapeDtypeStruct
    return pl.pallas_call(
        forward_kernel,
        in_specs=[SMEM] + [ANY] * 4 + [VMEM, ANY],
        out_specs=[ANY] * 3 + [VMEM] * 5,
        out_shape=[shape((N, C), BF16), shape((N, C), F32), shape((N, 128), F32)]
        + [shape((Q, H), BF16)] * 4
        + [shape((N, H), F32)],
        scratch_shapes=[
            pltpu.VMEM((4, Q, C), BF16),
            pltpu.VMEM((6 * Q, C), BF16),
            pltpu.VMEM((3, C, H), BF16),
            pltpu.VMEM((N, C), F32),
            pltpu.VMEM((N, 128), F32),
            pltpu.SemaphoreType.DMA((3,)),
            pltpu.SemaphoreType.DMA((4,)),
            pltpu.SemaphoreType.DMA((3,)),
        ],
        compiler_params=params(56),
        cost_estimate=cost(6 * N * C * H, 20_000_000),
        name="forward",
    )(odd, pieces[0], pieces[3], pieces[1], pieces[2], gain, weights)


def pre_grad_kernel(me_ref, core_ref, grad_ref, slope_ref, all_ref, kept_ref, away_ref):
    me, core = me_ref[0], core_ref[0]
    for k in range(4):
        at = slice(k * Q, (k + 1) * Q)
        grad = grad_ref[lax.bitwise_xor(me, k)].astype(F32)
        value = (grad * slope_ref[at, :]).astype(BF16)
        all_ref[at, :] = value
        low, high = value[:, :HALF], value[:, HALF:]
        kept_ref[at, :] = jnp.where(core == 0, low, high)
        away_ref[at, :] = jnp.where(core == 0, high, low)


def pre_grads(me, core, grads, slope):
    shape = jax.ShapeDtypeStruct
    return pl.pallas_call(
        pre_grad_kernel,
        in_specs=[SMEM] * 2 + [VMEM] * 2,
        out_specs=[VMEM] * 3,
        out_shape=[shape((N, H), BF16), shape((N, HALF), BF16), shape((N, HALF), BF16)],
        compiler_params=params(56),
        cost_estimate=cost(30_000_000_000, 5_000_000),
        name="pre_grads",
    )(me, core, grads, slope)


def backward_kernel(
    odd_ref, grad_ref, p0, p1, p2, p3, gain_ref, slope_hbm, inv_hbm, weights_ref,
    b0, b1, b2, b3, share_ref,
    ring, held, total, slope_ref, inv_ref, rows_in, sems, in_sems,
):
    copies = taps_in(odd_ref, weights_ref, held, sems)
    copies = [copies[1], copies[0], copies[2]]
    for copy in copies:
        copy.start()
    ins = [
        pltpu.make_async_copy(slope_hbm, slope_ref, in_sems.at[0]),
        pltpu.make_async_copy(inv_hbm, inv_ref, in_sems.at[1]),
    ] + [
        pltpu.make_async_copy(source, rows_in.at[k], in_sems.at[2 + k])
        for k, source in enumerate((p0, p1, p2, p3))
    ]
    for copy in ins:
        copy.start()
    ring[Q:5 * Q] = grad_ref[...]
    ring[:Q] = grad_ref[3 * Q:]
    ring[5 * Q:] = grad_ref[:Q]
    for i, copy in enumerate(copies):
        copy.wait()
        tap = (1, 0, 2)[i]
        first = (1, 2, 0)[i] * Q
        for n in range(6):
            cols = slice(n * 256, (n + 1) * 256)
            value = contract_cols(ring[first:first + N], held[tap, cols])
            total[:, cols] = value if i == 0 else total[:, cols] + value
    for copy in ins:
        copy.wait()
    step = 64
    share = jnp.zeros((8, C), F32)
    for k, out in enumerate((b0, b1, b2, b3)):

        def some(i, share, k=k, out=out):
            at = pl.ds(pl.multiple_of(i * step, step), step)
            here = pl.ds(pl.multiple_of(k * Q + i * step, step), step)
            inv = inv_ref[here, :1]
            hat = rows_in[k, at, :].astype(F32) * inv
            norm_grad = total[here, :] * slope_ref[here, :]
            product = norm_grad * hat
            mean = jnp.mean(product * gain_ref[...], axis=-1, keepdims=True)
            out[at, :] = ((norm_grad * gain_ref[...] - hat * mean) * inv).astype(BF16)
            return share + product.reshape(step // 8, 8, C).sum(0)

        share = lax.fori_loop(0, Q // step, some, share)
    share_ref[...] = jnp.sum(share, axis=0, keepdims=True)


def backward(odd, grads, pieces, gain, slope, inv, weights):
    shape = jax.ShapeDtypeStruct
    return pl.pallas_call(
        backward_kernel,
        in_specs=[SMEM, VMEM] + [ANY] * 4 + [VMEM] + [ANY] * 3,
        out_specs=[VMEM] * 5,
        out_shape=[shape((Q, C), BF16)] * 4 + [shape((1, C), F32)],
        scratch_shapes=[
            pltpu.VMEM((6 * Q, H), BF16),
            pltpu.VMEM((3, C, H), BF16),
            pltpu.VMEM((N, C), F32),
            pltpu.VMEM((N, C), F32),
            pltpu.VMEM((N, 128), F32),
            pltpu.VMEM((4, Q, C), BF16),
            pltpu.SemaphoreType.DMA((3,)),
            pltpu.SemaphoreType.DMA((6,)),
        ],
        compiler_params=params(56),
        cost_estimate=cost(1_000_000, 100_000),
        name="backward",
    )(odd, grads, *pieces, gain, slope, inv, weights)


def load_columns(own_hbm, other_hbm, both, sems):
    ins = []
    for i in range(4):
        cols = pl.ds(i * HALF, HALF)
        ins.append((
            pltpu.make_async_copy(own_hbm.at[:, cols], both.at[i, pl.ds(0, N)], sems.at[2 * i]),
            pltpu.make_async_copy(other_hbm.at[:, cols], both.at[i, pl.ds(N, N)], sems.at[2 * i + 1]),
        ))
        for copy in ins[-1]:
            copy.start()
    return ins


def kernel_share_kernel(
    odd_ref, own_hbm, other_hbm, kept_ref, came_ref, out_ref,
    both, right, rings, value, ring_sems, in_sems, out_sems,
):
    rows_in = [
        pltpu.make_async_copy(source, rings.at[i, pl.ds(Q, N)], ring_sems.at[i])
        for i, source in enumerate((kept_ref, came_ref))
    ]
    for copy in rows_in:
        copy.start()
    ins = load_columns(own_hbm, other_hbm, both, in_sems)
    odd = odd_ref[0]
    near = pl.multiple_of(jnp.where(odd == 0, 2 * Q, 0), Q)
    far = pl.multiple_of(jnp.where(odd == 0, 0, 2 * Q), Q)
    for i in range(2):
        rows_in[i].wait()
        rings[i, :Q] = rings[i, 4 * Q:5 * Q]
        rings[i, 5 * Q:] = rings[i, Q:2 * Q]
        rows = slice(i * N, (i + 1) * N)
        right[rows, :HALF] = rings[i, pl.ds(near, N), :]
        right[rows, HALF:2 * HALF] = rings[i, Q:5 * Q]
        right[rows, 2 * HALF:] = rings[i, pl.ds(far, N), :]
    outs = []
    for i in range(4):
        for copy in ins[i]:
            copy.wait()
        part = contract_rows(both[i], right[...]).astype(BF16)
        for b in range(9):
            value[2 * i:2 * i + 2, :, 48 * b:48 * b + 48, :] = part[
                :, 128 * b:128 * b + 128
            ].reshape(2, 4, 48, 128)
        for g in (2 * i, 2 * i + 1):
            outs.append(
                pltpu.make_async_copy(value.at[g], out_ref.at[:, g], out_sems.at[g])
            )
            outs[-1].start()
    for copy in outs:
        copy.wait()


def kernel_shares(odd, own, other, kept, came):
    return pl.pallas_call(
        kernel_share_kernel,
        in_specs=[SMEM] + [ANY] * 4,
        out_specs=ANY,
        out_shape=jax.ShapeDtypeStruct((4, 8, 432, 128), BF16),
        scratch_shapes=[
            pltpu.VMEM((4, 2 * N, HALF), BF16),
            pltpu.VMEM((2 * N, 3 * HALF), BF16),
            pltpu.VMEM((2, 6 * Q, HALF), BF16),
            pltpu.VMEM((8, 4, 432, 128), BF16),
            pltpu.SemaphoreType.DMA((2,)),
            pltpu.SemaphoreType.DMA((8,)),
            pltpu.SemaphoreType.DMA((8,)),
        ],
        compiler_params=params(56),
        cost_estimate=cost(6 * N * C * H, 10_000_000),
        name="kernel_shares",
    )(odd, own, other, kept, came)


def point_share_kernel(
    z_ref, me_ref, own_hbm, other_hbm, kept_ref, came_ref, gain_ref, d0, d1, d2, d3,
    both, right, value, in_sems, out_sems,
):
    ins = []
    for i in range(4):
        cols = pl.ds(i * HALF, HALF)
        ins.append([
            pltpu.make_async_copy(
                source.at[home_rows(me_ref, k), cols],
                both.at[i, pl.ds(side * N + k * Q, Q)],
                in_sems.at[8 * i + 4 * side + k],
            )
            for side, source in enumerate((own_hbm, other_hbm))
            for k in range(4)
        ])
        for copy in ins[-1]:
            copy.start()
    value[:, :, 144:] = gain_ref[...]
    right[:N] = kept_ref[...]
    right[N:] = came_ref[...]
    outs = []
    for i in range(4):
        for copy in ins[i]:
            copy.wait()
        part = contract_rows(both[i], right[...]).astype(BF16)
        for b in range(3):
            value[2 * i:2 * i + 2, :, 48 * b:48 * b + 48, :] = part[
                :, 128 * b:128 * b + 128
            ].reshape(2, 4, 48, 128)
        for g in (2 * i, 2 * i + 1):
            for d, out in enumerate((d0, d1, d2, d3)):
                source = value.at[g, lax.rem(z_ref[0] + d, 4)]
                outs.append(pltpu.make_async_copy(source, out.at[g], out_sems.at[len(outs)]))
                outs[-1].start()
    for copy in outs:
        copy.wait()


def point_shares(z, me, own, other, kept, came, gain):
    return pl.pallas_call(
        point_share_kernel,
        in_specs=[SMEM, SMEM, ANY, ANY, VMEM, VMEM, VMEM],
        out_specs=[ANY] * 4,
        out_shape=[jax.ShapeDtypeStruct((8, 160, 128), BF16)] * 4,
        scratch_shapes=[
            pltpu.VMEM((4, 2 * N, HALF), BF16),
            pltpu.VMEM((2 * N, HALF), BF16),
            pltpu.VMEM((8, 4, 160, 128), BF16),
            pltpu.SemaphoreType.DMA((32,)),
            pltpu.SemaphoreType.DMA((32,)),
        ],
        compiler_params=params(56),
        cost_estimate=cost(2 * N * C * H, 6_000_000),
        name="point_shares",
    )(z, me, own, other, kept, came, gain)


def four_sum(a, b, c, d):
    return ((a.astype(F32) + b.astype(F32)) + (c.astype(F32) + d.astype(F32))).astype(BF16)


def tap_sum_kernel(shares_ref, out_ref):
    out_ref[...] = four_sum(*[shares_ref[i] for i in range(4)])


def tap_sums(shares):
    return pl.pallas_call(
        tap_sum_kernel,
        grid=(4,),
        in_specs=[pl.BlockSpec((4, 2, 432, 128), lambda g: (0, g, 0, 0))],
        out_specs=pl.BlockSpec((2, 432, 128), lambda g: (g, 0, 0)),
        out_shape=jax.ShapeDtypeStruct((8, 432, 128), BF16),
        compiler_params=params(32),
        cost_estimate=cost(3_000_000, 5_000_000),
        name="tap_sums",
    )(shares)


def plane_kernel(taps_ref, d0, d1, d2, d3, out_ref):
    point = four_sum(d0[...], d1[...], d2[...], d3[...])
    out_ref[:, 0, :288] = taps_ref[:, :288]
    out_ref[:, 1, :144] = taps_ref[:, 288:]
    out_ref[:, 1, 144:288] = point[:, :144]
    for chip in range(2):
        out_ref[:, chip, 288:] = point[:, 144:]


def plane_shares(taps, points):
    return pl.pallas_call(
        plane_kernel,
        in_specs=[VMEM] * 5,
        out_specs=VMEM,
        out_shape=jax.ShapeDtypeStruct((8, 2, 304, 128), BF16),
        compiler_params=params(32),
        cost_estimate=cost(1_000_000, 3_000_000),
        name="plane_shares",
    )(taps, *points)


def mid_half_kernel(core_ref, m0, m1, m2, m3, kept_ref, away_ref):
    core = core_ref[0]
    for k, source in enumerate((m0, m1, m2, m3)):
        at = slice(k * Q, (k + 1) * Q)
        low, high = source[:, :HALF], source[:, HALF:]
        kept_ref[at, :] = jnp.where(core == 0, low, high)
        away_ref[at, :] = jnp.where(core == 0, high, low)


def mid_halves(core, mid):
    shape = jax.ShapeDtypeStruct
    return pl.pallas_call(
        mid_half_kernel,
        in_specs=[SMEM] + [VMEM] * 4,
        out_specs=[VMEM] * 2,
        out_shape=[shape((N, HALF), BF16)] * 2,
        compiler_params=params(56),
        cost_estimate=cost(N * H, 2_000_000),
        name="mid_halves",
    )(core, *mid)


def unpack_kernel(whole_ref, kernel_ref, point_ref, gain_ref):
    for core in range(2):
        for b in range(3):
            cols = slice(core * HALF + b * 128, core * HALF + b * 128 + 128)
            first, second = slice(48 * b, 48 * b + 48), slice(144 + 48 * b, 192 + 48 * b)
            kernel_ref[0, :, cols] = whole_ref[core, first]
            kernel_ref[1, :, cols] = whole_ref[core, second]
            kernel_ref[2, :, cols] = whole_ref[2 + core, first]
            point_ref[:, cols] = whole_ref[2 + core, second]
    gain_ref[...] = whole_ref[0, 288:296] + whole_ref[1, 288:296]


def unpacked(whole):
    shape = jax.ShapeDtypeStruct
    return pl.pallas_call(
        unpack_kernel,
        in_specs=[VMEM],
        out_specs=[VMEM] * 3,
        out_shape=[shape((3, 48, H), F32), shape((48, H), F32), shape((8, 128), F32)],
        compiler_params=params(32),
        cost_estimate=cost(1_000_000, 1_200_000),
        name="unpack",
    )(whole)


def home_rows(me_ref, k):
    return pl.ds(pl.multiple_of(lax.bitwise_xor(me_ref[0], k) * Q, Q), Q)


def stream_out_kernel(
    me_ref, m0, m1, m2, m3, point_ref, stream_ref, out_ref,
    mid, point, rows, result, in_sems, out_sems,
):
    ins = [pltpu.make_async_copy(point_ref, point, in_sems.at[8])]
    for k, source in enumerate((m0, m1, m2, m3)):
        at = pl.ds(k * Q, Q)
        ins.append(pltpu.make_async_copy(source, mid.at[at], in_sems.at[k]))
        ins.append(
            pltpu.make_async_copy(stream_ref.at[home_rows(me_ref, k)], rows.at[at], in_sems.at[4 + k])
        )
    for copy in ins:
        copy.start()
    for copy in ins:
        copy.wait()
    for n in range(6):
        cols = slice(n * 256, (n + 1) * 256)
        result[:, cols] = (rows[:, cols].astype(F32) + dot(mid[...], point[:, cols])).astype(BF16)
    outs = [
        pltpu.make_async_copy(
            result.at[pl.ds(k * Q, Q)], out_ref.at[home_rows(me_ref, k)], out_sems.at[k]
        )
        for k in range(4)
    ]
    for copy in outs:
        copy.start()
    for copy in outs:
        copy.wait()


def home_stream_out(me, mid, point_kernel, stream):
    return pl.pallas_call(
        stream_out_kernel,
        in_specs=[SMEM] + [ANY] * 6,
        out_specs=ANY,
        out_shape=jax.ShapeDtypeStruct((N, C), BF16),
        scratch_shapes=[
            pltpu.VMEM((N, H), BF16),
            pltpu.VMEM((H, C), BF16),
            pltpu.VMEM((N, C), BF16),
            pltpu.VMEM((N, C), BF16),
            pltpu.SemaphoreType.DMA((9,)),
            pltpu.SemaphoreType.DMA((4,)),
        ],
        compiler_params=params(56),
        cost_estimate=cost(2 * N * C * H, 6_000_000),
        name="stream_out",
    )(me, *mid, point_kernel, stream)


def stream_grad_kernel(
    me_ref, b0, b1, b2, b3, cotan_ref, out_ref, back, rows, in_sems, out_sems
):
    ins = []
    for k, source in enumerate((b0, b1, b2, b3)):
        ins.append((
            pltpu.make_async_copy(source, back.at[k], in_sems.at[k]),
            pltpu.make_async_copy(cotan_ref.at[home_rows(me_ref, k)], rows.at[k], in_sems.at[4 + k]),
        ))
        for copy in ins[-1]:
            copy.start()
    outs = []
    for k in range(4):
        for copy in ins[k]:
            copy.wait()
        rows[k] = (rows[k].astype(F32) + back[k].astype(F32)).astype(BF16)
        outs.append(
            pltpu.make_async_copy(rows.at[k], out_ref.at[home_rows(me_ref, k)], out_sems.at[k])
        )
        outs[-1].start()
    for copy in outs:
        copy.wait()


def home_stream_grad(me, back, cotan):
    return pl.pallas_call(
        stream_grad_kernel,
        in_specs=[SMEM] + [ANY] * 5,
        out_specs=ANY,
        out_shape=jax.ShapeDtypeStruct((N, C), BF16),
        scratch_shapes=[
            pltpu.VMEM((4, Q, C), BF16),
            pltpu.VMEM((4, Q, C), BF16),
            pltpu.SemaphoreType.DMA((8,)),
            pltpu.SemaphoreType.DMA((4,)),
        ],
        compiler_params=params(56),
        cost_estimate=cost(2 * N * C, 5_000_000),
        name="stream_grad",
    )(me, *back, cotan)


def swap_core(value):
    return lax.ppermute(value, "core", [(0, 1), (1, 0)])


def partner(value, k):
    return lax.ppermute(value, GROUP, [(i, i ^ k) for i in range(4)])


def exchange(pieces):
    return [pieces[0]] + [partner(pieces[k], k) for k in range(1, len(pieces))]


def shards(stream, norm_gain_vector, conv_kernel, point_kernel, out_grad):
    core = lax.axis_index("core").astype(jnp.int32)
    odd = lax.axis_index("yh").astype(jnp.int32)
    me = 2 * lax.axis_index("xh") + odd
    z = lax.axis_index("z").astype(jnp.int32)
    core_word, odd_word, z_word = core.reshape(1), odd.reshape(1), z.reshape(1)
    gain_row = norm_gain_vector.reshape(1, C)
    cotan = out_grad[0]

    me_word = me.reshape(1)
    quarters = stream[0].reshape(4, Q, C)
    pieces = exchange([lax.dynamic_index_in_dim(quarters, me ^ k, 0, False) for k in range(4)])
    mid_grad = contract_cols(cotan, point_kernel).astype(BF16).reshape(4, Q, H)
    _, *pieces = lax.optimization_barrier((mid_grad, *pieces))
    mid_grad = lax.all_to_all(mid_grad, GROUP, 0, 0, tiled=True)
    cotan_other = swap_core(cotan)

    act, slope_in, inv, m0, m1, m2, m3, slope = forward(
        odd_word, pieces, gain_row, conv_kernel
    )
    mid_grad, slope = lax.optimization_barrier((mid_grad, slope))
    pre_grad, kept, away = pre_grads(me_word, core_word, mid_grad, slope)
    act_other = swap_core(act)
    came = swap_core(away)
    shares = kernel_shares(odd_word, act, act_other, kept, came)
    shares, pre_grad, m0, m1, m2, m3 = lax.optimization_barrier(
        (shares, pre_grad, m0, m1, m2, m3)
    )
    shares = lax.all_to_all(shares, "z", 0, 0, tiled=True)
    mid = exchange([m0, m1, m2, m3])
    b0, b1, b2, b3, gain = backward(
        odd_word, pre_grad, pieces, gain_row, slope_in, inv, conv_kernel
    )
    back = exchange([b0, b1, b2, b3])
    gain, *mid = lax.optimization_barrier((gain, *mid))
    mid_kept, mid_away = mid_halves(core_word, mid)
    mid_came = swap_core(mid_away)
    gain = gain.astype(BF16).reshape(8, 4, 1, 48)
    gain = jnp.pad(gain, ((0, 0), (0, 0), (0, 15), (0, 80)))
    points = list(
        point_shares(z_word, me_word, cotan, cotan_other, mid_kept, mid_came, gain)
    )
    points[0], points[1], points[2], points[3], back[1], *mid = lax.optimization_barrier(
        (*points, back[1], *mid)
    )
    points = [points[0]] + [
        lax.ppermute(points[d], "z", [(i, (i + d) % 4) for i in range(4)]) for d in (1, 2, 3)
    ]
    stream_out = home_stream_out(me_word, mid, point_kernel, stream[0])
    shares, stream_out = lax.optimization_barrier((shares, stream_out))
    taps = tap_sums(shares)
    stream_grad = home_stream_grad(me_word, back, cotan)
    taps, stream_grad, *points = lax.optimization_barrier((taps, stream_grad, *points))
    plane = plane_shares(taps, points).reshape(16, 304, 128)
    plane = lax.all_to_all(plane, PLANE, 0, 0, tiled=True)
    plane = jnp.sum(plane.astype(F32), axis=0)[:296]
    whole = lax.all_gather(plane, ("xl", "core"))
    kernel_grad, point_grad, gain_grad = unpacked(whole)
    return (stream_out[None], stream_grad[None], kernel_grad, point_grad.T, gain_grad[0, :48])


def solution(mesh):
    fine = Mesh(
        mesh.devices.reshape(2, 2, 2, 4, 2, 2), ("xh", "yh", "yl", "z", "xl", "core")
    )
    ctx, rep = ("xh", "yh", "yl", "z"), ("xl", "core")
    placed = (P(rep, ctx, None), P(), P(), P(), P(rep, ctx, None))
    return jax.shard_map(
        shards,
        mesh=fine,
        in_specs=placed,
        out_specs=(
            P(rep, ctx, None),
            P(rep, ctx, None),
            P(None, ctx, None),
            P(None, ctx),
            P(ctx),
        ),
        check_vma=False,
    )
```
